512 devices in a mesh: ia: 32 (over x_lo, y, core), ja: 16 (over x_hi, z).
Axes of the slice: x: 4 (x_hi: 2, x_lo: 2; x = x_hi * 2 + x_lo), y: 8, z: 8, core: 2. Of those that a mesh axis runs over, the one named last changes fastest.
Arguments:
- pair: bfloat16 [384, 384, 128], P('ia', 'ja'), may hold values from -6 to 6
- token_mask: int32 [384], replicated, may hold values 0 or 1
- norm_in_gain: float32 [128], replicated, may hold values from 0.1 to 1.9
- norm_in_bias: float32 [128], replicated, may hold values from -3 to 3
- left_gate: bfloat16 [128, 128], replicated, may hold values from -0.5 to 0.5
- left_value: bfloat16 [128, 128], replicated, may hold values from -0.5 to 0.5
- right_gate: bfloat16 [128, 128], replicated, may hold values from -0.5 to 0.5
- right_value: bfloat16 [128, 128], replicated, may hold values from -0.5 to 0.5
- output_gate: bfloat16 [128, 128], replicated, may hold values from -0.5 to 0.5
- norm_out_gain: float32 [128], replicated, may hold values from 0.1 to 1.9
- norm_out_bias: float32 [128], replicated, may hold values from -3 to 3
- output_weight: bfloat16 [128, 128], replicated, may hold values from -0.5 to 0.5
Outputs:
- update: bfloat16 [384, 384, 128], P('ia', 'ja')
The draws below stay inside these ranges and needn't reach their ends.
All inputs are finite; a program needn't handle non-finite values.
Results may differ from the reference program's by a relative error of at most 0.0054.
Values may be sent and summed in bfloat16 or wider, within the bound.
No kernel may reach another device: no remote copies, remote signals or barrier semaphores. Data moves between devices by JAX's collectives and lax.ppermute only.
A program may use at most 64 MiB of HBM per device.

```python
import jax
import jax.numpy as jnp
from jax import lax

C = 128
CH = 128
N = 384


def set_ends(result, rng, low, high):
    place = [jax.random.randint(jax.random.fold_in(rng, axis), (), 0, length) for axis, length in enumerate(result.shape)]
    main_axis = result.shape.index(max(result.shape))
    neighbour = place[:main_axis] + [(place[main_axis] + 1) % result.shape[main_axis]] + place[main_axis + 1:]
    return result.at[tuple(place)].set(low).at[tuple(neighbour)].set(high)


def block_scale(key, shape, pieces, low, top_value):
    level = 1.0
    for axis_at, parts in pieces:
        steps = jax.random.uniform(jax.random.fold_in(jax.random.fold_in(key, 6), axis_at), (parts,), jnp.float32, low / len(pieces), top_value / len(pieces))
        level = level * jnp.repeat(jnp.exp(steps), shape[axis_at] // parts).reshape((-1,) + (1,) * (len(shape) - 1 - axis_at))
    return level


def bell_draw(stream_key, extent, scale, most, pieces=(), held_as=jnp.bfloat16):
    result = scale * jax.random.normal(stream_key, extent, jnp.float32)
    if pieces:
        result = result * block_scale(stream_key, extent, pieces, -0.22, 0.18)
    return jnp.clip(result, -most, most).astype(held_as)


def setup_inputs(seed: int = 0) -> dict:
    streams_of = jax.random.split(jax.random.key(seed), 13)
    pair = bell_draw(streams_of[0], (N, N, C), 1.0, 6.0, ((0, 32), (1, 16)))
    token_mask = set_ends((jax.random.randint(streams_of[1], (N,), 0, 8) < 7).astype(jnp.int32), jax.random.fold_in(streams_of[1], 1), 0, 1)
    norm_in_gain = jnp.clip(1.0 + 0.18 * jax.random.normal(streams_of[2], (C,), jnp.float32), 0.1, 1.9)
    norm_in_bias = bell_draw(streams_of[3], (C,), 0.5, 3.0, (), jnp.float32)
    left_gate = bell_draw(streams_of[4], (C, CH), C ** -0.5, 0.5)
    left_value = bell_draw(streams_of[5], (C, CH), C ** -0.5, 0.5)
    right_gate = bell_draw(streams_of[6], (C, CH), C ** -0.5, 0.5)
    right_value = bell_draw(streams_of[7], (C, CH), C ** -0.5, 0.5)
    output_gate = bell_draw(streams_of[8], (C, C), C ** -0.5, 0.5)
    norm_out_gain = jnp.clip(1.0 + 0.18 * jax.random.normal(streams_of[9], (CH,), jnp.float32), 0.1, 1.9)
    norm_out_bias = bell_draw(streams_of[10], (CH,), 0.5, 3.0, (), jnp.float32)
    output_weight = bell_draw(streams_of[11], (CH, C), CH ** -0.5, 0.5)
    return dict(pair=pair, token_mask=token_mask, norm_in_gain=norm_in_gain, norm_in_bias=norm_in_bias, left_gate=left_gate, left_value=left_value, right_gate=right_gate, right_value=right_value, output_gate=output_gate, norm_out_gain=norm_out_gain, norm_out_bias=norm_out_bias, output_weight=output_weight)


def layer_norm(values, gain, bias):
    mean = lax.optimization_barrier(jnp.mean(values, axis=-1, keepdims=True))
    centered = values - mean
    variance = lax.optimization_barrier(jnp.mean(centered * centered, axis=-1, keepdims=True))
    return centered * jax.lax.rsqrt(variance + 1e-05) * gain + bias

def project(normed, weight):
    return jnp.einsum('ijc,cd->ijd', normed.astype(jnp.float32), weight.astype(jnp.float32))

def reference(pair, token_mask, norm_in_gain, norm_in_bias, left_gate, left_value, right_gate, right_value, output_gate, norm_out_gain, norm_out_bias, output_weight):
    normed = layer_norm(pair.astype(jnp.float32), norm_in_gain, norm_in_bias).astype(jnp.bfloat16)
    valid = token_mask.astype(jnp.float32)
    pair_mask = (valid[:, None] * valid[None, :])[:, :, None]
    left = (pair_mask * jax.nn.sigmoid(project(normed, left_gate)) * project(normed, left_value)).astype(jnp.bfloat16)
    right = (pair_mask * jax.nn.sigmoid(project(normed, right_gate)) * project(normed, right_value)).astype(jnp.bfloat16)
    mixed = jnp.einsum('ikc,jkc->ijc', left.astype(jnp.float32), right.astype(jnp.float32))
    mixed_normed = layer_norm(mixed, norm_out_gain, norm_out_bias).astype(jnp.bfloat16)
    gated = jax.nn.sigmoid(project(normed, output_gate))
    return (gated * project(mixed_normed, output_weight)).astype(jnp.bfloat16)
```

```python
import jax
import jax.numpy as jnp
import numpy as np
from jax import lax
from jax.experimental import pallas as pl
from jax.experimental.pallas import tpu as pltpu
from jax.sharding import Mesh
from jax.sharding import PartitionSpec as P

AXES = ("xl", "y2", "y1", "y0", "c", "xh", "z2", "z1", "z0")
ROWS = ("xl", "y2", "y1", "y0", "c")
COLS = ("xh", "z2", "z1", "z0")
NEAR = ("xl", "y0", "c", "xh", "z0")
EPS = 1e-5
WIDE = 32
F32 = jnp.float32
BF16 = jnp.bfloat16
VMEM = pl.BlockSpec(memory_space=pltpu.VMEM)
SMEM = pl.BlockSpec(memory_space=pltpu.SMEM)


def sigmoid(x):
    return 1.0 / (1.0 + jnp.exp(-x))


def iota(shape, axis):
    return lax.broadcasted_iota(jnp.int32, shape, axis)


def contract(a, b, da, db):
    return lax.dot_general(a, b, (((da,), (db,)), ((), ())), preferred_element_type=F32)


def edges_kernel(place_ref, mask_ref, pair_ref, gain_ref, bias_ref, lg_ref, lv_ref, rg_ref, rv_ref, og_ref, sent_ref, gate_ref):
    rows, cols, width = pair_ref.shape
    x = pair_ref[...].astype(F32).reshape(rows * cols, width)
    mean = jnp.mean(x, axis=-1, keepdims=True)
    centered = x - mean
    variance = jnp.mean(centered * centered, axis=-1, keepdims=True)
    normed = centered * lax.rsqrt(variance + EPS) * gain_ref[...] + bias_ref[...]
    rounded = normed.astype(BF16)
    gate_ref[...] = sigmoid(contract(rounded, og_ref[...], 1, 0))
    place = iota((cols, width), 0)
    col_valid = jnp.zeros((cols, width), F32)
    for k in range(cols):
        col_valid = jnp.where(place == k, mask_ref[place_ref[1] + k].astype(F32), col_valid)
    parts = []
    for i in range(rows):
        row_valid = mask_ref[place_ref[0] + i].astype(F32)
        parts.append(normed[i * cols : (i + 1) * cols] * (col_valid * row_valid))
        parts.append(jnp.zeros((WIDE - cols, width), F32))
    masked = jnp.concatenate(parts, axis=0).astype(BF16)
    left = sigmoid(contract(lg_ref[...], masked, 0, 1)) * contract(lv_ref[...], masked, 0, 1)
    right = sigmoid(contract(rg_ref[...], masked, 0, 1)) * contract(rv_ref[...], masked, 0, 1)
    lanes = rows * WIDE
    left = left.reshape(width // 8, 8, lanes)
    right = right.reshape(width // 8, 8, lanes)
    low = iota((1, 8, lanes), 1) < 4
    even = jnp.where(low, left, pltpu.roll(right, 4, 1))
    odd = jnp.where(low, pltpu.roll(left, 4, 1), right)
    for t in range(width // 8):
        sent_ref[2 * t] = even[t].astype(BF16)
        sent_ref[2 * t + 1] = odd[t].astype(BF16)


def swap_blocks(blocks, lane):
    out = []
    for b in range(4):
        total = None
        for a in range(4):
            moved = blocks[a] if a == b else pltpu.roll(blocks[a], (WIDE * (a - b)) % 128, blocks[a].ndim - 1)
            total = moved if total is None else jnp.where(lane // WIDE == a, moved, total)
        out.append(total)
    return out


def arrange_kernel(got_ref, left_ref, right_ref, rows_ref):
    lane = iota((8, 128), 1)
    for g in range(8):
        for q in range(3):
            blocks = [got_ref[g * 4 + kg, :, q * 128 : (q + 1) * 128].astype(F32) for kg in range(4)]
            for ii, block in enumerate(swap_blocks(blocks, lane)):
                rows_ref[pl.ds((g * 12 + q * 4 + ii) * 8, 8), :] = block
    for c in range(4):
        left = rows_ref[pl.ds(c, 96, stride=8), :].astype(BF16)
        for copy in range(4):
            left_ref[copy, c] = left
        right_ref[c] = rows_ref[pl.ds(4 + c, 96, stride=8), :].astype(BF16)


def mix_kernel(place_ref, left_ref, r0_ref, r1_ref, r2_ref, r3_ref, sent_ref, wide_ref, rows_ref):
    lane = iota((96, 128), 1)
    wide_ref[...] = jnp.zeros((96, 128), F32)
    for c in range(4):
        mixed = None
        for s, r_ref in enumerate((r0_ref, r1_ref, r2_ref, r3_ref)):
            part = contract(left_ref[lax.rem(place_ref[2] + 4 - s, 4), c], r_ref[c], 1, 1)
            mixed = part if mixed is None else mixed + part
        wide_ref[:, 0:96] = mixed
        flat = wide_ref[...]
        spread = flat
        for jg in range(1, 4):
            spread = jnp.where(lane // WIDE == jg, pltpu.roll(flat, 8 * jg, 1), spread)
        spread = jnp.where(lane % WIDE < 24, spread, 0.0)
        high = spread.astype(BF16).astype(F32)
        rows_ref[pl.ds(c, 96, stride=8), :] = high
        rows_ref[pl.ds(4 + c, 96, stride=8), :] = spread - high
    lane = iota((8, 128), 1)
    for g in range(8):
        for q in range(3):
            blocks = [rows_ref[pl.ds((g * 12 + q * 4 + ii) * 8, 8), :] for ii in range(4)]
            for jg, block in enumerate(swap_blocks(blocks, lane)):
                sent_ref[g * 4 + jg, :, q * 128 : (q + 1) * 128] = block.astype(BF16)


def update_kernel(got_ref, gate_ref, gain_ref, bias_ref, weight_ref, out_ref):
    rows, cols, width = out_ref.shape
    lanes = rows * WIDE
    low = iota((8, lanes), 0) < 4
    tiles = []
    for t in range(width // 8):
        pair = []
        for p in (2 * t, 2 * t + 1):
            both = got_ref[p].astype(F32)
            pair.append(both + pltpu.roll(both, 4, 0))
        tiles.append(jnp.where(low, pair[0], pair[1]))
    mixed = jnp.concatenate(tiles, axis=0)
    mean = jnp.mean(mixed, axis=0, keepdims=True)
    centered = mixed - mean
    variance = jnp.mean(centered * centered, axis=0, keepdims=True)
    gain = jnp.transpose(jnp.broadcast_to(gain_ref[...], (width, width)))[:, 0:1]
    bias = jnp.transpose(jnp.broadcast_to(bias_ref[...], (width, width)))[:, 0:1]
    normed = (centered * lax.rsqrt(variance + EPS) * gain + bias).astype(BF16)
    output = contract(normed, weight_ref[...], 0, 0)
    for i in range(rows):
        gated = gate_ref[i * cols : (i + 1) * cols] * output[i * WIDE : i * WIDE + cols]
        out_ref[i] = gated.astype(BF16)


def shards(
    pair,
    token_mask,
    norm_in_gain,
    norm_in_bias,
    left_gate,
    left_value,
    right_gate,
    right_value,
    output_gate,
    norm_out_gain,
    norm_out_bias,
    output_weight,
):
    rows, cols, width = pair.shape
    params = pltpu.CompilerParams(vmem_limit_bytes=32 * 1024 * 1024)
    row_block = lax.axis_index(("y2", "y1"))
    place = jnp.stack([lax.axis_index(ROWS) * rows, lax.axis_index(COLS) * cols, row_block, row_block]).astype(jnp.int32)
    struct = jax.ShapeDtypeStruct
    sent, gate = pl.pallas_call(
        edges_kernel,
        name="edges",
        out_shape=(struct((32, 8, rows * WIDE), BF16), struct((rows * cols, width), F32)),
        in_specs=[SMEM, SMEM] + [VMEM] * 8,
        out_specs=(VMEM, VMEM),
        compiler_params=params,
    )(place, token_mask, pair, norm_in_gain.reshape(1, -1), norm_in_bias.reshape(1, -1), left_gate, left_value, right_gate, right_value, output_gate)
    got = lax.all_to_all(sent, NEAR, 0, 0)
    left, right = pl.pallas_call(
        arrange_kernel,
        name="arrange",
        out_shape=(struct((4, 4, 96, 128), BF16), struct((4, 96, 128), BF16)),
        in_specs=[VMEM],
        out_specs=(VMEM, VMEM),
        scratch_shapes=[pltpu.VMEM((768, 128), F32)],
        compiler_params=params,
    )(got)
    lefts = lax.all_to_all(left, ("z2", "z1"), 0, 0)
    rights = []
    for shift in range(4):
        moves = [(y * 4 + z, ((z + shift) % 4) * 4 + y) for y in range(4) for z in range(4)]
        rights.append(lax.ppermute(right, ("y2", "y1", "z2", "z1"), moves))
    sent = pl.pallas_call(
        mix_kernel,
        name="mix",
        out_shape=struct((32, 8, rows * WIDE), BF16),
        in_specs=[SMEM] + [VMEM] * 5,
        out_specs=VMEM,
        scratch_shapes=[pltpu.VMEM((96, 128), F32), pltpu.VMEM((768, 128), F32)],
        compiler_params=params,
    )(place, lefts, *rights)
    got = lax.all_to_all(sent, NEAR, 0, 0)
    return pl.pallas_call(
        update_kernel,
        name="update",
        out_shape=struct((rows, cols, width), BF16),
        in_specs=[VMEM] * 5,
        out_specs=VMEM,
        compiler_params=params,
    )(got, gate, norm_out_gain.reshape(1, -1), norm_out_bias.reshape(1, -1), output_weight)


def solution(mesh):
    fine = Mesh(np.asarray(mesh.devices).reshape((2,) * len(AXES)), AXES)
    placed = (P(ROWS, COLS, None),) + (P(),) * 11
    return jax.shard_map(shards, mesh=fine, in_specs=placed, out_specs=P(ROWS, COLS, None), check_vma=False)
```

```python
import jax
import jax.numpy as jnp
import numpy as np
from jax import lax
from jax.experimental import pallas as pl
from jax.experimental.pallas import tpu as pltpu
from jax.sharding import Mesh
from jax.sharding import PartitionSpec as P

AXES = ("xl", "y2", "y1", "y0", "c", "xh", "z2", "z1", "z0")
ROWS = ("xl", "y2", "y1", "y0", "c")
COLS = ("xh", "z2", "z1", "z0")
NEAR = ("xl", "y0", "c", "xh", "z0")
EPS = 1e-5
WIDE = 32
F32 = jnp.float32
BF16 = jnp.bfloat16
VMEM = pl.BlockSpec(memory_space=pltpu.VMEM)
SMEM = pl.BlockSpec(memory_space=pltpu.SMEM)
HBM = pl.BlockSpec(memory_space=pltpu.HBM)


def sigmoid(x):
    return 1.0 / (1.0 + jnp.exp(-x))


def iota(shape, axis):
    return lax.broadcasted_iota(jnp.int32, shape, axis)


def contract(a, b, da, db):
    return lax.dot_general(a, b, (((da,), (db,)), ((), ())), preferred_element_type=F32)


def edges_kernel(
    place_ref,
    mask_ref,
    pair_ref,
    gain_ref,
    bias_ref,
    out_gain_ref,
    out_bias_ref,
    lg_hbm,
    lv_hbm,
    rg_hbm,
    rv_hbm,
    og_hbm,
    sent_ref,
    gate_ref,
    columns_ref,
    weights_ref,
    arrived,
):
    copies = []
    for n, source in enumerate((og_hbm, lg_hbm, lv_hbm, rg_hbm, rv_hbm)):
        copies.append(pltpu.make_async_copy(source, weights_ref.at[n], arrived.at[n]))
        copies[n].start()
    rows, cols, width = pair_ref.shape
    x = pair_ref[...].astype(F32).reshape(rows * cols, width)
    mean = jnp.mean(x, axis=-1, keepdims=True)
    centered = x - mean
    variance = jnp.mean(centered * centered, axis=-1, keepdims=True)
    normed = centered * lax.rsqrt(variance + EPS) * gain_ref[...] + bias_ref[...]
    rounded = normed.astype(BF16)
    columns_ref[0] = jnp.transpose(jnp.broadcast_to(out_gain_ref[...], (width, width)))
    columns_ref[1] = jnp.transpose(jnp.broadcast_to(out_bias_ref[...], (width, width)))
    place = iota((cols, width), 0)
    col_valid = jnp.zeros((cols, width), F32)
    for k in range(cols):
        col_valid = jnp.where(place == k, mask_ref[place_ref[1] + k].astype(F32), col_valid)
    parts = []
    for i in range(rows):
        row_valid = mask_ref[place_ref[0] + i].astype(F32)
        parts.append(normed[i * cols : (i + 1) * cols] * (col_valid * row_valid))
        parts.append(jnp.zeros((WIDE - cols, width), F32))
    masked = jnp.concatenate(parts, axis=0).astype(BF16)
    for copy in copies:
        copy.wait()
    gate_ref[...] = sigmoid(contract(rounded, weights_ref[0], 1, 0))
    left = sigmoid(contract(weights_ref[1], masked, 0, 1)) * contract(weights_ref[2], masked, 0, 1)
    right = sigmoid(contract(weights_ref[3], masked, 0, 1)) * contract(weights_ref[4], masked, 0, 1)
    lanes = rows * WIDE
    left = left.reshape(width // 8, 8, lanes)
    right = right.reshape(width // 8, 8, lanes)
    low = iota((1, 8, lanes), 1) < 4
    even = jnp.where(low, left, pltpu.roll(right, 4, 1))
    odd = jnp.where(low, pltpu.roll(left, 4, 1), right)
    for t in range(width // 8):
        sent_ref[2 * t] = even[t].astype(BF16)
        sent_ref[2 * t + 1] = odd[t].astype(BF16)


def swap_blocks(blocks, lane):
    out = []
    for b in range(4):
        total = None
        for a in range(4):
            moved = blocks[a] if a == b else pltpu.roll(blocks[a], (WIDE * (a - b)) % 128, blocks[a].ndim - 1)
            total = moved if total is None else jnp.where(lane // WIDE == a, moved, total)
        out.append(total)
    return out


def arrange_kernel(got_ref, left_ref, right_ref, rows_ref):
    lane = iota((8, 128), 1)
    for g in range(8):
        for q in range(3):
            blocks = [got_ref[g * 4 + kg, :, q * 128 : (q + 1) * 128].astype(F32) for kg in range(4)]
            for ii, block in enumerate(swap_blocks(blocks, lane)):
                rows_ref[pl.ds((g * 12 + q * 4 + ii) * 8, 8), :] = block
    wide = iota((96, 128), 1) % WIDE < 24
    for side in range(2):
        found = [rows_ref[pl.ds(4 * side + c, 96, stride=8), :] for c in range(4)]
        for v in range(3):
            dense = jnp.where(wide, found[v], pltpu.roll(found[3], 24 - 8 * v, 1)).astype(BF16)
            if side == 0:
                for copy in range(4):
                    left_ref[copy, :, v * 128 : (v + 1) * 128] = dense
            else:
                right_ref[:, v * 128 : (v + 1) * 128] = dense


def mix_kernel(left_ref, right_ref, sent_ref, wide_ref, rows_ref):
    lane = iota((96, 128), 1)
    wide_ref[...] = jnp.zeros((96, 128), F32)
    for c in range(4):
        mixed = None
        for s in range(4):
            for v in (c,) if c < 3 else (0, 1, 2):
                held = (lane % WIDE < 24) if c < 3 else (lane % WIDE >= 24)
                left = left_ref[s, :, v * 128 : (v + 1) * 128]
                left = jnp.where(held, left, jnp.zeros_like(left))
                part = contract(left, right_ref[s, :, v * 128 : (v + 1) * 128], 1, 1)
                mixed = part if mixed is None else mixed + part
        wide_ref[:, 0:96] = mixed
        flat = wide_ref[...]
        spread = flat
        for jg in range(1, 4):
            spread = jnp.where(lane // WIDE == jg, pltpu.roll(flat, 8 * jg, 1), spread)
        spread = jnp.where(lane % WIDE < 24, spread, 0.0)
        high = spread.astype(BF16).astype(F32)
        rows_ref[pl.ds(c, 96, stride=8), :] = high
        rows_ref[pl.ds(4 + c, 96, stride=8), :] = spread - high
    lane = iota((8, 128), 1)
    for g in range(8):
        for q in range(3):
            blocks = [rows_ref[pl.ds((g * 12 + q * 4 + ii) * 8, 8), :] for ii in range(4)]
            for jg, block in enumerate(swap_blocks(blocks, lane)):
                sent_ref[g * 4 + jg, :, q * 128 : (q + 1) * 128] = block.astype(BF16)


def update_kernel(got_ref, gate_ref, columns_ref, weight_ref, out_ref):
    rows, cols, width = out_ref.shape
    lanes = rows * WIDE
    low = iota((8, lanes), 0) < 4
    tiles = []
    for t in range(width // 8):
        pair = []
        for p in (2 * t, 2 * t + 1):
            both = got_ref[p].astype(F32)
            pair.append(both + pltpu.roll(both, 4, 0))
        tiles.append(jnp.where(low, pair[0], pair[1]))
    mixed = jnp.concatenate(tiles, axis=0)
    mean = jnp.mean(mixed, axis=0, keepdims=True)
    centered = mixed - mean
    variance = jnp.mean(centered * centered, axis=0, keepdims=True)
    normed = (centered * lax.rsqrt(variance + EPS) * columns_ref[0][:, 0:1] + columns_ref[1][:, 0:1]).astype(BF16)
    output = contract(normed, weight_ref[...], 0, 0)
    for i in range(rows):
        gated = gate_ref[i * cols : (i + 1) * cols] * output[i * WIDE : i * WIDE + cols]
        out_ref[i] = gated.astype(BF16)


def shards(
    pair,
    token_mask,
    norm_in_gain,
    norm_in_bias,
    left_gate,
    left_value,
    right_gate,
    right_value,
    output_gate,
    norm_out_gain,
    norm_out_bias,
    output_weight,
):
    rows, cols, width = pair.shape
    params = pltpu.CompilerParams(vmem_limit_bytes=32 * 1024 * 1024)
    place = jnp.stack([lax.axis_index(ROWS) * rows, lax.axis_index(COLS) * cols]).astype(jnp.int32)
    struct = jax.ShapeDtypeStruct
    sent, gate, columns = pl.pallas_call(
        edges_kernel,
        name="edges",
        out_shape=(
            struct((32, 8, rows * WIDE), BF16),
            struct((rows * cols, width), F32),
            struct((2, width, width), F32),
        ),
        in_specs=[SMEM, SMEM] + [VMEM] * 5 + [HBM] * 5,
        out_specs=(VMEM, VMEM, VMEM),
        scratch_shapes=[pltpu.VMEM((5, width, width), BF16), pltpu.SemaphoreType.DMA((5,))],
        compiler_params=params,
    )(
        place,
        token_mask,
        pair,
        norm_in_gain.reshape(1, -1),
        norm_in_bias.reshape(1, -1),
        norm_out_gain.reshape(1, -1),
        norm_out_bias.reshape(1, -1),
        left_gate,
        left_value,
        right_gate,
        right_value,
        output_gate,
    )
    got = lax.all_to_all(sent, NEAR, 0, 0)
    left, right = pl.pallas_call(
        arrange_kernel,
        name="arrange",
        out_shape=(struct((4, 96, 384), BF16), struct((96, 384), BF16)),
        in_specs=[VMEM],
        out_specs=(VMEM, VMEM),
        scratch_shapes=[pltpu.VMEM((768, 128), F32)],
        compiler_params=params,
    )(got)
    lefts = lax.all_to_all(left, ("z2", "z1"), 0, 0)
    right = lax.ppermute(right, ("y2", "y1", "z2", "z1"), [(y * 4 + z, z * 4 + y) for y in range(4) for z in range(4)])
    rights = lax.all_to_all(jnp.broadcast_to(right, (4, 96, 384)), ("y2", "y1"), 0, 0)
    sent = pl.pallas_call(
        mix_kernel,
        name="mix",
        out_shape=struct((32, 8, rows * WIDE), BF16),
        in_specs=[VMEM] * 2,
        out_specs=VMEM,
        scratch_shapes=[pltpu.VMEM((96, 128), F32), pltpu.VMEM((768, 128), F32)],
        compiler_params=params,
    )(lefts, rights)
    got = lax.all_to_all(sent, NEAR, 0, 0)
    return pl.pallas_call(
        update_kernel,
        name="update",
        out_shape=struct((rows, cols, width), BF16),
        in_specs=[VMEM] * 4,
        out_specs=VMEM,
        compiler_params=params,
    )(got, gate, columns, output_weight)


def solution(mesh):
    fine = Mesh(np.asarray(mesh.devices).reshape((2,) * len(AXES)), AXES)
    placed = (P(ROWS, COLS, None),) + (P(),) * 11
    return jax.shard_map(shards, mesh=fine, in_specs=placed, out_specs=P(ROWS, COLS, None), check_vma=False)
```

```python
import jax
import jax.numpy as jnp
from jax import lax
from jax.experimental import pallas as pl
from jax.experimental.pallas import tpu as pltpu
from jax.sharding import PartitionSpec as P

BOTH = ("ia", "ja")
EPS = 1e-5
WIDE = 32
F32 = jnp.float32
BF16 = jnp.bfloat16
VMEM = pl.BlockSpec(memory_space=pltpu.VMEM)
SMEM = pl.BlockSpec(memory_space=pltpu.SMEM)


def device(xl, y, core, xh, z):
    return (((xl * 8 + y) * 2 + core) * 2 + xh) * 8 + z


def fold(half, m):
    return m if half == 0 else 7 - m


SHARING = [
    [device(xl, fold(half, m), core, xh, z) for xl in range(2) for m in range(4) for xh in range(2) for z in range(8)]
    for half in range(2)
    for core in range(2)
]
SAME = [[group[n] for group in SHARING] for n in range(128)]


def sigmoid(x):
    return 1.0 / (1.0 + jnp.exp(-x))


def iota(shape, axis):
    return lax.broadcasted_iota(jnp.int32, shape, axis)


def contract(a, b, da, db):
    return lax.dot_general(a, b, (((da,), (db,)), ((), ())), preferred_element_type=F32)


def norm_kernel(place_ref, mask_ref, pair_ref, gain_ref, bias_ref, out_gain_ref, out_bias_ref, normed_ref, masked_ref, columns_ref):
    rows, cols, width = pair_ref.shape
    x = pair_ref[...].astype(F32).reshape(rows * cols, width)
    mean = jnp.mean(x, axis=-1, keepdims=True)
    centered = x - mean
    variance = jnp.mean(centered * centered, axis=-1, keepdims=True)
    normed = centered * lax.rsqrt(variance + EPS) * gain_ref[...] + bias_ref[...]
    normed_ref[...] = normed.astype(BF16)
    columns_ref[0] = jnp.transpose(jnp.broadcast_to(out_gain_ref[...], (width, width)))
    columns_ref[1] = jnp.transpose(jnp.broadcast_to(out_bias_ref[...], (width, width)))
    place = iota((cols, width), 0)
    col_valid = jnp.zeros((cols, width), F32)
    for k in range(cols):
        col_valid = jnp.where(place == k, mask_ref[place_ref[1] + k].astype(F32), col_valid)
    parts = []
    for i in [3 * ii + iq for iq in range(3) for ii in range(4)]:
        row_valid = mask_ref[place_ref[0] + i].astype(F32)
        parts.append(normed[i * cols : (i + 1) * cols] * (col_valid * row_valid))
        parts.append(jnp.zeros((WIDE - cols, width), F32))
    masked_ref[...] = jnp.concatenate(parts, axis=0).astype(BF16)


def edges_kernel(normed_ref, masked_ref, lg_ref, lv_ref, rg_ref, rv_ref, og_ref, sent_ref, gate_ref, rows_ref):
    width = lg_ref.shape[0]
    masked = masked_ref[...]
    left = sigmoid(contract(lg_ref[...], masked, 0, 1)) * contract(lv_ref[...], masked, 0, 1)
    right = sigmoid(contract(rg_ref[...], masked, 0, 1)) * contract(rv_ref[...], masked, 0, 1)
    for iq in range(3):
        rows_ref[pl.ds(iq, width, stride=8), :] = right[:, iq * 128 : (iq + 1) * 128]
        rows_ref[pl.ds(3 + iq, width, stride=8), :] = left[:, iq * 128 : (iq + 1) * 128]
    for iq in range(6, 8):
        rows_ref[pl.ds(iq, width, stride=8), :] = jnp.zeros((width, 128), F32)
    sent_ref[...] = rows_ref[...].reshape(width, 8, 128).astype(BF16)
    gate_ref[...] = sigmoid(contract(normed_ref[...], og_ref[...], 1, 0))


def swap_blocks(blocks, lane):
    out = []
    for b in range(4):
        total = None
        for a in range(4):
            moved = blocks[a] if a == b else pltpu.roll(blocks[a], (WIDE * (a - b)) % 128, blocks[a].ndim - 1)
            total = moved if total is None else jnp.where(lane // WIDE == a, moved, total)
        out.append(total)
    return out


def arrange_kernel(got_ref, left_ref, right_ref, rows_ref, padded_ref):
    lane = iota((8, 128), 1)
    padded_ref[...] = jnp.zeros_like(padded_ref)
    for g in range(8):
        for quad in range(4):
            blocks = [got_ref[g * 16 + quad * 4 + k].astype(F32) for k in range(4)]
            for ii, block in enumerate(swap_blocks(blocks, lane)):
                rows_ref[quad, pl.ds((g * 4 + ii) * 8, 8), :] = block
                padded_ref[quad, pl.ds(g * 16 + ii * 3, 3), :] = block[0:3]
    wide = iota((32, 128), 1) % WIDE < 24
    for iq in range(3):
        found = [rows_ref[quad, pl.ds(3 + iq, 32, stride=8), :] for quad in range(4)]
        for v in range(3):
            dense = jnp.where(wide, found[v], pltpu.roll(found[3], 24 - 8 * v, 1))
            left_ref[iq * 32 : (iq + 1) * 32, v * 128 : (v + 1) * 128] = dense.astype(BF16)
    wide = iota((128, 128), 1) % WIDE < 24
    for v in range(3):
        dense = jnp.where(wide, padded_ref[v], pltpu.roll(padded_ref[3], 24 - 8 * v, 1)).astype(BF16)
        for copy in range(4):
            right_ref[copy, :, v * 128 : (v + 1) * 128] = dense


def mix_kernel(left_ref, right_ref, sent_ref, rows_ref):
    lane = iota((8, 128), 1)
    left = left_ref[...]
    for quad in range(4):
        pieces = []
        for k in range(quad * 4, quad * 4 + 4):
            xl, y = k // 8, k % 8
            half, m = (0, y) if y < 4 else (1, 7 - y)
            at = (xl * 4 + m) * 16
            for core in range(2):
                pieces.append(right_ref[half * 2 + core, at : at + 16, :])
        mixed = contract(left, jnp.concatenate(pieces, axis=0), 1, 1)
        high = mixed.astype(BF16).astype(F32)
        low = mixed - high
        for iq in range(3):
            rows_ref[pl.ds(iq, 32, stride=8), :] = high[iq * 32 : (iq + 1) * 32]
            rows_ref[pl.ds(3 + iq, 32, stride=8), :] = low[iq * 32 : (iq + 1) * 32]
        for iq in range(6, 8):
            rows_ref[pl.ds(iq, 32, stride=8), :] = jnp.zeros((32, 128), F32)
        for g in range(8):
            blocks = [rows_ref[pl.ds((g * 4 + ii) * 8, 8), :] for ii in range(4)]
            for k, block in enumerate(swap_blocks(blocks, lane)):
                sent_ref[g * 16 + quad * 4 + k] = block.astype(BF16)


def update_kernel(got_ref, gate_ref, columns_ref, weight_ref, out_ref, rows_ref, flat_ref):
    rows, cols, width = out_ref.shape
    rows_ref[...] = got_ref[...].astype(F32).reshape(width * 8, 128)
    gain = columns_ref[0][:, 0:1]
    bias = columns_ref[1][:, 0:1]
    for iq in range(3):
        mixed = rows_ref[pl.ds(iq, width, stride=8), :] + rows_ref[pl.ds(3 + iq, width, stride=8), :]
        mean = jnp.mean(mixed, axis=0, keepdims=True)
        centered = mixed - mean
        variance = jnp.mean(centered * centered, axis=0, keepdims=True)
        normed = (centered * lax.rsqrt(variance + EPS) * gain + bias).astype(BF16)
        output = contract(normed, weight_ref[...], 0, 0)
        for ii in range(4):
            at = (3 * ii + iq) * cols
            flat_ref[at : at + 12, :] = output[ii * WIDE : ii * WIDE + 12]
            flat_ref[at + 12 : at + 24, :] = output[ii * WIDE + 16 : ii * WIDE + 28]
    out_ref[...] = (gate_ref[...] * flat_ref[...]).astype(BF16).reshape(rows, cols, width)


def shards(
    pair,
    token_mask,
    norm_in_gain,
    norm_in_bias,
    left_gate,
    left_value,
    right_gate,
    right_value,
    output_gate,
    norm_out_gain,
    norm_out_bias,
    output_weight,
):
    rows, cols, width = pair.shape
    params = pltpu.CompilerParams(vmem_limit_bytes=32 * 1024 * 1024)
    place = jnp.stack([lax.axis_index("ia") * rows, lax.axis_index("ja") * cols]).astype(jnp.int32)
    struct = jax.ShapeDtypeStruct
    normed, masked, columns = pl.pallas_call(
        norm_kernel,
        name="norm",
        out_shape=(
            struct((rows * cols, width), BF16),
            struct((rows * WIDE, width), BF16),
            struct((2, width, width), F32),
        ),
        in_specs=[SMEM, SMEM] + [VMEM] * 5,
        out_specs=(VMEM, VMEM, VMEM),
        compiler_params=params,
    )(
        place,
        token_mask,
        pair,
        norm_in_gain.reshape(1, -1),
        norm_in_bias.reshape(1, -1),
        norm_out_gain.reshape(1, -1),
        norm_out_bias.reshape(1, -1),
    )
    sent, gate = pl.pallas_call(
        edges_kernel,
        name="edges",
        out_shape=(struct((128, 8, 128), BF16), struct((rows * cols, width), F32)),
        in_specs=[VMEM] * 7,
        out_specs=(VMEM, VMEM),
        scratch_shapes=[pltpu.VMEM((1024, 128), F32)],
        compiler_params=params,
    )(normed, masked, left_gate, left_value, right_gate, right_value, output_gate)
    got = lax.all_to_all(sent, BOTH, 0, 0, axis_index_groups=SHARING)
    left, right = pl.pallas_call(
        arrange_kernel,
        name="arrange",
        out_shape=(struct((96, 384), BF16), struct((4, 128, 384), BF16)),
        in_specs=[VMEM],
        out_specs=(VMEM, VMEM),
        scratch_shapes=[pltpu.VMEM((4, 256, 128), F32), pltpu.VMEM((4, 128, 128), F32)],
        compiler_params=params,
    )(got)
    rights = lax.all_to_all(right, BOTH, 0, 0, axis_index_groups=SAME)
    sent = pl.pallas_call(
        mix_kernel,
        name="mix",
        out_shape=struct((128, 8, 128), BF16),
        in_specs=[VMEM] * 2,
        out_specs=VMEM,
        scratch_shapes=[pltpu.VMEM((256, 128), F32)],
        compiler_params=params,
    )(left, rights)
    got = lax.all_to_all(sent, BOTH, 0, 0, axis_index_groups=SHARING)
    return pl.pallas_call(
        update_kernel,
        name="update",
        out_shape=struct((rows, cols, width), BF16),
        in_specs=[VMEM] * 4,
        out_specs=VMEM,
        scratch_shapes=[pltpu.VMEM((1024, 128), F32), pltpu.VMEM((rows * cols, 128), F32)],
        compiler_params=params,
    )(got, gate, columns, output_weight)


def solution(mesh):
    placed = (P("ia", "ja", None),) + (P(),) * 11
    return jax.shard_map(shards, mesh=mesh, in_specs=placed, out_specs=P("ia", "ja", None), check_vma=False)
```

```python
import jax
import jax.numpy as jnp
from jax import lax
from jax.experimental import pallas as pl
from jax.experimental.pallas import tpu as pltpu
from jax.sharding import PartitionSpec as P

BOTH = ("ia", "ja")
EPS = 1e-5
WIDE = 32
NORM_BYTES = 32 * 1024 * 1024
F32 = jnp.float32
BF16 = jnp.bfloat16
VMEM = pl.BlockSpec(memory_space=pltpu.VMEM)
SMEM = pl.BlockSpec(memory_space=pltpu.SMEM)


def device(xl, y, core, xh, z):
    return (((xl * 8 + y) * 2 + core) * 2 + xh) * 8 + z


def fold(half, m):
    return m if half == 0 else 7 - m


SHARING = [
    [device(xl, fold(half, m), core, xh, z) for xl in range(2) for m in range(4) for xh in range(2) for z in range(8)]
    for half in range(2)
    for core in range(2)
]
PLACES = [(xl, y, core, xh, z) for xl in range(2) for y in range(8) for core in range(2) for xh in range(2) for z in range(8)]
CORE_FLIP = [(device(xl, y, core, xh, z), device(xl, y, 1 - core, xh, z)) for xl, y, core, xh, z in PLACES]
HALF_FLIP = [(device(xl, y, core, xh, z), device(xl, 7 - y, core, xh, z)) for xl, y, core, xh, z in PLACES]


def sigmoid(x):
    return 1.0 / (1.0 + jnp.exp(-x))


def iota(shape, axis):
    return lax.broadcasted_iota(jnp.int32, shape, axis)


def contract(a, b, da, db):
    return lax.dot_general(a, b, (((da,), (db,)), ((), ())), preferred_element_type=F32)


def norm_kernel(place_ref, mask_ref, pair_ref, gain_ref, bias_ref, normed_ref, masked_ref):
    rows, cols, width = pair_ref.shape
    x = pair_ref[...].astype(F32).reshape(rows * cols, width)
    mean = jnp.mean(x, axis=-1, keepdims=True)
    centered = x - mean
    variance = jnp.mean(centered * centered, axis=-1, keepdims=True)
    normed = centered * lax.rsqrt(variance + EPS) * gain_ref[...] + bias_ref[...]
    normed_ref[...] = normed.astype(BF16)
    place = iota((cols, width), 0)
    col_valid = jnp.zeros((cols, width), F32)
    for k in range(cols):
        col_valid = jnp.where(place == k, mask_ref[place_ref[1] + k].astype(F32), col_valid)
    parts = []
    for i in [3 * ii + iq for iq in range(3) for ii in range(4)]:
        row_valid = mask_ref[place_ref[0] + i].astype(F32)
        parts.append(normed[i * cols : (i + 1) * cols] * (col_valid * row_valid))
        parts.append(jnp.zeros((WIDE - cols, width), F32))
    masked_ref[...] = jnp.concatenate(parts, axis=0).astype(BF16)


def edges_kernel(
    masked_ref,
    lg_ref,
    lv_ref,
    rg_ref,
    rv_ref,
    out_gain_ref,
    out_bias_ref,
    sent_ref,
    columns_ref,
    rows_ref,
):
    width = lg_ref.shape[0]
    columns_ref[0] = jnp.transpose(jnp.broadcast_to(out_gain_ref[...], (width, width)))
    columns_ref[1] = jnp.transpose(jnp.broadcast_to(out_bias_ref[...], (width, width)))
    masked = masked_ref[...]
    left = sigmoid(contract(lg_ref[...], masked, 0, 1)) * contract(lv_ref[...], masked, 0, 1)
    right = sigmoid(contract(rg_ref[...], masked, 0, 1)) * contract(rv_ref[...], masked, 0, 1)
    for iq in range(3):
        rows_ref[pl.ds(iq, width, stride=8), :] = right[:, iq * 128 : (iq + 1) * 128]
        rows_ref[pl.ds(3 + iq, width, stride=8), :] = left[:, iq * 128 : (iq + 1) * 128]
    for iq in range(6, 8):
        rows_ref[pl.ds(iq, width, stride=8), :] = jnp.zeros((width, 128), F32)
    sent_ref[...] = rows_ref[...].reshape(width, 8, 128).astype(BF16)


def swap_blocks(blocks, lane):
    out = []
    for b in range(4):
        total = None
        for a in range(4):
            moved = blocks[a] if a == b else pltpu.roll(blocks[a], (WIDE * (a - b)) % 128, blocks[a].ndim - 1)
            total = moved if total is None else jnp.where(lane // WIDE == a, moved, total)
        out.append(total)
    return out


def arrange_kernel(got_ref, left_ref, right_ref, rows_ref, padded_ref):
    lane = iota((8, 128), 1)
    padded_ref[...] = jnp.zeros_like(padded_ref)
    for g in range(8):
        for quad in range(4):
            blocks = [got_ref[g * 16 + quad * 4 + k].astype(F32) for k in range(4)]
            for ii, block in enumerate(swap_blocks(blocks, lane)):
                rows_ref[quad, pl.ds((g * 4 + ii) * 8, 8), :] = block
                padded_ref[quad, pl.ds(g * 16 + ii * 3, 3), :] = block[0:3]
    wide = iota((32, 128), 1) % WIDE < 24
    for iq in range(3):
        found = [rows_ref[quad, pl.ds(3 + iq, 32, stride=8), :] for quad in range(4)]
        for v in range(3):
            dense = jnp.where(wide, found[v], pltpu.roll(found[3], 24 - 8 * v, 1))
            left_ref[iq * 32 : (iq + 1) * 32, v * 128 : (v + 1) * 128] = dense.astype(BF16)
    wide = iota((128, 128), 1) % WIDE < 24
    for v in range(3):
        dense = jnp.where(wide, padded_ref[v], pltpu.roll(padded_ref[3], 24 - 8 * v, 1))
        right_ref[:, v * 128 : (v + 1) * 128] = dense.astype(BF16)


def mix_kernel(place_ref, left_ref, own_ref, near_ref, far_ref, both_ref, sent_ref, rows_ref):
    lane = iota((8, 128), 1)
    left = left_ref[...]
    core = place_ref[2]
    for other in range(2):
        mine, theirs = ((own_ref, near_ref), (far_ref, both_ref))[other]
        mine, theirs = mine[...], theirs[...]
        first = jnp.where(core == 0, mine, theirs)
        second = jnp.where(core == 0, theirs, mine)
        half = place_ref[3 + other]
        for xl in range(2):
            pieces = []
            for m in range(4):
                at = (xl * 4 + m) * 16
                pieces += [first[at : at + 16], second[at : at + 16]]
            mixed = contract(left, jnp.concatenate(pieces, axis=0), 1, 1)
            high = mixed.astype(BF16).astype(F32)
            low = mixed - high
            for iq in range(3):
                rows_ref[pl.ds(iq, 32, stride=8), :] = high[iq * 32 : (iq + 1) * 32]
                rows_ref[pl.ds(3 + iq, 32, stride=8), :] = low[iq * 32 : (iq + 1) * 32]
            for iq in range(6, 8):
                rows_ref[pl.ds(iq, 32, stride=8), :] = jnp.zeros((32, 128), F32)
            for g in range(8):
                blocks = [rows_ref[pl.ds((g * 4 + ii) * 8, 8), :] for ii in range(4)]
                for m, block in enumerate(swap_blocks(blocks, lane)):
                    sent_ref[g * 16 + xl * 8 + m + half * (7 - 2 * m)] = block.astype(BF16)


def update_kernel(got_ref, normed_ref, gate_ref, columns_ref, weight_ref, out_ref, rows_ref, flat_ref):
    rows, cols, width = out_ref.shape
    rows_ref[...] = got_ref[...].astype(F32).reshape(width * 8, 128)
    gain = columns_ref[0][:, 0:1]
    bias = columns_ref[1][:, 0:1]
    for iq in range(3):
        mixed = rows_ref[pl.ds(iq, width, stride=8), :] + rows_ref[pl.ds(3 + iq, width, stride=8), :]
        mean = jnp.mean(mixed, axis=0, keepdims=True)
        centered = mixed - mean
        variance = jnp.mean(centered * centered, axis=0, keepdims=True)
        normed = (centered * lax.rsqrt(variance + EPS) * gain + bias).astype(BF16)
        output = contract(normed, weight_ref[...], 0, 0)
        for ii in range(4):
            at = (3 * ii + iq) * cols
            flat_ref[at : at + 12, :] = output[ii * WIDE : ii * WIDE + 12]
            flat_ref[at + 12 : at + 24, :] = output[ii * WIDE + 16 : ii * WIDE + 28]
    gated = sigmoid(contract(normed_ref[...], gate_ref[...], 1, 0))
    out_ref[...] = (gated * flat_ref[...]).astype(BF16).reshape(rows, cols, width)


def shards(
    pair,
    token_mask,
    norm_in_gain,
    norm_in_bias,
    left_gate,
    left_value,
    right_gate,
    right_value,
    output_gate,
    norm_out_gain,
    norm_out_bias,
    output_weight,
):
    rows, cols, width = pair.shape
    params = pltpu.CompilerParams(vmem_limit_bytes=32 * 1024 * 1024)
    row_block = lax.axis_index("ia")
    half = row_block // 8 % 2
    place = jnp.stack([row_block * rows, lax.axis_index("ja") * cols, row_block % 2, half, 1 - half]).astype(jnp.int32)
    struct = jax.ShapeDtypeStruct
    normed, masked = pl.pallas_call(
        norm_kernel,
        name="norm",
        out_shape=(struct((rows * cols, width), BF16), struct((rows * WIDE, width), BF16)),
        in_specs=[SMEM, SMEM] + [VMEM] * 3,
        out_specs=(VMEM, VMEM),
        compiler_params=params,
        cost_estimate=pl.CostEstimate(flops=0, bytes_accessed=NORM_BYTES, transcendentals=0),
    )(place, token_mask, pair, norm_in_gain.reshape(1, -1), norm_in_bias.reshape(1, -1))
    sent, columns = pl.pallas_call(
        edges_kernel,
        name="edges",
        out_shape=(
            struct((128, 8, 128), BF16),
            struct((2, width, width), F32),
        ),
        in_specs=[VMEM] * 7,
        out_specs=(VMEM, VMEM),
        scratch_shapes=[pltpu.VMEM((1024, 128), F32)],
        compiler_params=params,
    )(
        masked,
        left_gate,
        left_value,
        right_gate,
        right_value,
        norm_out_gain.reshape(1, -1),
        norm_out_bias.reshape(1, -1),
    )
    got = lax.all_to_all(sent, BOTH, 0, 0, axis_index_groups=SHARING)
    left, right = pl.pallas_call(
        arrange_kernel,
        name="arrange",
        out_shape=(struct((96, 384), BF16), struct((128, 384), BF16)),
        in_specs=[VMEM],
        out_specs=(VMEM, VMEM),
        scratch_shapes=[pltpu.VMEM((4, 256, 128), F32), pltpu.VMEM((4, 128, 128), F32)],
        compiler_params=params,
    )(got)
    near = lax.ppermute(right, BOTH, CORE_FLIP)
    far = lax.ppermute(right, BOTH, HALF_FLIP)
    both = lax.ppermute(far, BOTH, CORE_FLIP)
    sent = pl.pallas_call(
        mix_kernel,
        name="mix",
        out_shape=struct((128, 8, 128), BF16),
        in_specs=[SMEM] + [VMEM] * 5,
        out_specs=VMEM,
        scratch_shapes=[pltpu.VMEM((256, 128), F32)],
        compiler_params=params,
    )(place, left, right, near, far, both)
    got = lax.all_to_all(sent, BOTH, 0, 0, axis_index_groups=SHARING)
    return pl.pallas_call(
        update_kernel,
        name="update",
        out_shape=struct((rows, cols, width), BF16),
        in_specs=[VMEM] * 5,
        out_specs=VMEM,
        scratch_shapes=[pltpu.VMEM((1024, 128), F32), pltpu.VMEM((rows * cols, 128), F32)],
        compiler_params=params,
    )(got, normed, output_gate, columns, output_weight)


def solution(mesh):
    placed = (P("ia", "ja", None),) + (P(),) * 11
    return jax.shard_map(shards, mesh=mesh, in_specs=placed, out_specs=P("ia", "ja", None), check_vma=False)
```

```python
import jax
import jax.numpy as jnp
from jax import lax
from jax.experimental import pallas as pl
from jax.experimental.pallas import tpu as pltpu
from jax.sharding import PartitionSpec as P

BOTH = ("ia", "ja")
EPS = 1e-5
WIDE = 32
NORM_BYTES = 32 * 1024 * 1024
F32 = jnp.float32
BF16 = jnp.bfloat16
VMEM = pl.BlockSpec(memory_space=pltpu.VMEM)
SMEM = pl.BlockSpec(memory_space=pltpu.SMEM)


def device(xl, y, core, xh, z):
    return (((xl * 8 + y) * 2 + core) * 2 + xh) * 8 + z


def fold(half, m):
    return m if half == 0 else 7 - m


SHARING = [
    [device(xl, fold(half, m), core, xh, z) for xl in range(2) for m in range(4) for xh in range(2) for z in range(8)]
    for half in range(2)
    for core in range(2)
]
PLACES = [(xl, y, core, xh, z) for xl in range(2) for y in range(8) for core in range(2) for xh in range(2) for z in range(8)]
CORE_FLIP = [(device(xl, y, core, xh, z), device(xl, y, 1 - core, xh, z)) for xl, y, core, xh, z in PLACES]
HALF_FLIP = [(device(xl, y, core, xh, z), device(xl, 7 - y, core, xh, z)) for xl, y, core, xh, z in PLACES]


def sigmoid(x):
    return 1.0 / (1.0 + jnp.exp(-x))


def iota(shape, axis):
    return lax.broadcasted_iota(jnp.int32, shape, axis)


def contract(a, b, da, db):
    return lax.dot_general(a, b, (((da,), (db,)), ((), ())), preferred_element_type=F32)


def norm_kernel(place_ref, mask_ref, pair_ref, gain_ref, bias_ref, normed_ref, masked_ref):
    rows, cols, width = pair_ref.shape
    x = pair_ref[...].astype(F32).reshape(rows * cols, width)
    mean = jnp.mean(x, axis=-1, keepdims=True)
    centered = x - mean
    variance = jnp.mean(centered * centered, axis=-1, keepdims=True)
    normed = centered * lax.rsqrt(variance + EPS) * gain_ref[...] + bias_ref[...]
    normed_ref[...] = normed.astype(BF16)
    place = iota((cols, width), 0)
    col_valid = jnp.zeros((cols, width), F32)
    for k in range(cols):
        col_valid = jnp.where(place == k, mask_ref[place_ref[1] + k].astype(F32), col_valid)
    parts = []
    for i in [3 * ii + iq for iq in range(3) for ii in range(4)]:
        row_valid = mask_ref[place_ref[0] + i].astype(F32)
        parts.append(normed[i * cols : (i + 1) * cols] * (col_valid * row_valid))
        parts.append(jnp.zeros((WIDE - cols, width), F32))
    masked_ref[...] = jnp.concatenate(parts, axis=0).astype(BF16)


def edges_kernel(
    masked_ref,
    lg_ref,
    lv_ref,
    rg_ref,
    rv_ref,
    out_gain_ref,
    out_bias_ref,
    sent_ref,
    columns_ref,
    rows_ref,
):
    width = lg_ref.shape[0]
    columns_ref[0] = jnp.transpose(jnp.broadcast_to(out_gain_ref[...], (width, width)))
    columns_ref[1] = jnp.transpose(jnp.broadcast_to(out_bias_ref[...], (width, width)))
    masked = masked_ref[...]
    left = sigmoid(contract(lg_ref[...], masked, 0, 1)) * contract(lv_ref[...], masked, 0, 1)
    right = sigmoid(contract(rg_ref[...], masked, 0, 1)) * contract(rv_ref[...], masked, 0, 1)
    for t in range(3):
        lanes = slice(t * 128, (t + 1) * 128)
        rows_ref[t, pl.ds(0, width, stride=2), :] = right[:, lanes]
        rows_ref[t, pl.ds(1, width, stride=2), :] = left[:, lanes]
        sent_ref[:, :, lanes] = rows_ref[t].astype(BF16).reshape(width, 2, 128)


def swap_blocks(blocks, lane):
    out = []
    for b in range(4):
        total = None
        for a in range(4):
            moved = blocks[a] if a == b else pltpu.roll(blocks[a], (WIDE * (a - b)) % 128, blocks[a].ndim - 1)
            total = moved if total is None else jnp.where(lane // WIDE == a, moved, total)
        out.append(total)
    return out


def arrange_kernel(got_ref, left_ref, right_ref, rows_ref, quads_ref, padded_ref):
    for t in range(3):
        rows_ref[t] = got_ref[:, :, t * 128 : (t + 1) * 128].astype(F32).reshape(256, 128)
    lane = iota((32, 128), 1)
    padded_ref[...] = jnp.zeros_like(padded_ref)
    wide = iota((8, 128), 1) % WIDE < 24
    for side in range(2):
        for iq in range(3):
            blocks = [rows_ref[iq, pl.ds(2 * k + side, 32, stride=8), :] for k in range(4)]
            done = []
            for ii, block in enumerate(swap_blocks(blocks, lane)):
                at = (side * 12 + iq * 4 + ii) * 32
                quads_ref[pl.ds(at, 32), :] = block
                found = [quads_ref[pl.ds(at + quad, 8, stride=4), :] for quad in range(4)]
                dense = [jnp.where(wide, found[v], pltpu.roll(found[3], 24 - 8 * v, 1)) for v in range(3)]
                done.append(dense)
                if side == 0:
                    for v in range(3):
                        padded_ref[v, pl.ds(ii * 3 + iq, 8, stride=16), :] = dense[v]
            if side == 1:
                for v in range(3):
                    block = jnp.concatenate([dense[v] for dense in done], axis=0)
                    left_ref[iq * 32 : (iq + 1) * 32, v * 128 : (v + 1) * 128] = block.astype(BF16)
    for v in range(3):
        right_ref[:, v * 128 : (v + 1) * 128] = padded_ref[v].astype(BF16)


def mix_kernel(place_ref, left_ref, own_ref, near_ref, far_ref, both_ref, sent_ref, rows_ref):
    lane = iota((8, 128), 1)
    left = left_ref[...]
    core = place_ref[2]
    for other in range(2):
        mine, theirs = ((own_ref, near_ref), (far_ref, both_ref))[other]
        mine, theirs = mine[...], theirs[...]
        first = jnp.where(core == 0, mine, theirs)
        second = jnp.where(core == 0, theirs, mine)
        half = place_ref[3 + other]
        for xl in range(2):
            pieces = []
            for m in range(4):
                at = (xl * 4 + m) * 16
                pieces += [first[at : at + 16], second[at : at + 16]]
            mixed = contract(left, jnp.concatenate(pieces, axis=0), 1, 1)
            high = mixed.astype(BF16).astype(F32)
            for part, values in enumerate((high, mixed - high)):
                for iq in range(3):
                    blocks = [values[(iq * 4 + ii) * 8 : (iq * 4 + ii + 1) * 8] for ii in range(4)]
                    for m, block in enumerate(swap_blocks(blocks, lane)):
                        to = (xl * 8 + m + half * (7 - 2 * m)) * 2 + part
                        rows_ref[iq, pl.ds(to, 8, stride=32), :] = block
    for t in range(3):
        sent_ref[:, :, t * 128 : (t + 1) * 128] = rows_ref[t].astype(BF16).reshape(128, 2, 128)


def update_kernel(got_ref, normed_ref, gate_ref, columns_ref, weight_ref, out_ref, rows_ref, flat_ref):
    rows, cols, width = out_ref.shape
    gain = columns_ref[0][:, 0:1]
    bias = columns_ref[1][:, 0:1]
    for iq in range(3):
        rows_ref[iq] = got_ref[:, :, iq * 128 : (iq + 1) * 128].astype(F32).reshape(2 * width, 128)
        mixed = rows_ref[iq, pl.ds(0, width, stride=2), :] + rows_ref[iq, pl.ds(1, width, stride=2), :]
        mean = jnp.mean(mixed, axis=0, keepdims=True)
        centered = mixed - mean
        variance = jnp.mean(centered * centered, axis=0, keepdims=True)
        normed = (centered * lax.rsqrt(variance + EPS) * gain + bias).astype(BF16)
        output = contract(normed, weight_ref[...], 0, 0)
        for ii in range(4):
            at = (3 * ii + iq) * cols
            flat_ref[at : at + 12, :] = output[ii * WIDE : ii * WIDE + 12]
            flat_ref[at + 12 : at + 24, :] = output[ii * WIDE + 16 : ii * WIDE + 28]
    gated = sigmoid(contract(normed_ref[...], gate_ref[...], 1, 0))
    out_ref[...] = (gated * flat_ref[...]).astype(BF16).reshape(rows, cols, width)


def shards(
    pair,
    token_mask,
    norm_in_gain,
    norm_in_bias,
    left_gate,
    left_value,
    right_gate,
    right_value,
    output_gate,
    norm_out_gain,
    norm_out_bias,
    output_weight,
):
    rows, cols, width = pair.shape
    params = pltpu.CompilerParams(vmem_limit_bytes=32 * 1024 * 1024)
    row_block = lax.axis_index("ia")
    half = row_block // 8 % 2
    place = jnp.stack([row_block * rows, lax.axis_index("ja") * cols, row_block % 2, half, 1 - half]).astype(jnp.int32)
    struct = jax.ShapeDtypeStruct
    normed, masked = pl.pallas_call(
        norm_kernel,
        name="norm",
        out_shape=(struct((rows * cols, width), BF16), struct((rows * WIDE, width), BF16)),
        in_specs=[SMEM, SMEM] + [VMEM] * 3,
        out_specs=(VMEM, VMEM),
        compiler_params=params,
        cost_estimate=pl.CostEstimate(flops=0, bytes_accessed=NORM_BYTES, transcendentals=0),
    )(place, token_mask, pair, norm_in_gain.reshape(1, -1), norm_in_bias.reshape(1, -1))
    sent, columns = pl.pallas_call(
        edges_kernel,
        name="edges",
        out_shape=(
            struct((128, 2, rows * WIDE), BF16),
            struct((2, width, width), F32),
        ),
        in_specs=[VMEM] * 7,
        out_specs=(VMEM, VMEM),
        scratch_shapes=[pltpu.VMEM((3, 256, 128), F32)],
        compiler_params=params,
    )(
        masked,
        left_gate,
        left_value,
        right_gate,
        right_value,
        norm_out_gain.reshape(1, -1),
        norm_out_bias.reshape(1, -1),
    )
    got = lax.all_to_all(sent, BOTH, 0, 0, axis_index_groups=SHARING)
    left, right = pl.pallas_call(
        arrange_kernel,
        name="arrange",
        out_shape=(struct((96, 384), BF16), struct((128, 384), BF16)),
        in_specs=[VMEM],
        out_specs=(VMEM, VMEM),
        scratch_shapes=[pltpu.VMEM((3, 256, 128), F32), pltpu.VMEM((768, 128), F32), pltpu.VMEM((3, 128, 128), F32)],
        compiler_params=params,
    )(got)
    near = lax.ppermute(right, BOTH, CORE_FLIP)
    far = lax.ppermute(right, BOTH, HALF_FLIP)
    both = lax.ppermute(far, BOTH, CORE_FLIP)
    sent = pl.pallas_call(
        mix_kernel,
        name="mix",
        out_shape=struct((128, 2, rows * WIDE), BF16),
        in_specs=[SMEM] + [VMEM] * 5,
        out_specs=VMEM,
        scratch_shapes=[pltpu.VMEM((3, 256, 128), F32)],
        compiler_params=params,
    )(place, left, right, near, far, both)
    got = lax.all_to_all(sent, BOTH, 0, 0, axis_index_groups=SHARING)
    return pl.pallas_call(
        update_kernel,
        name="update",
        out_shape=struct((rows, cols, width), BF16),
        in_specs=[VMEM] * 5,
        out_specs=VMEM,
        scratch_shapes=[pltpu.VMEM((3, 256, 128), F32), pltpu.VMEM((rows * cols, 128), F32)],
        compiler_params=params,
    )(got, normed, output_gate, columns, output_weight)


def solution(mesh):
    placed = (P("ia", "ja", None),) + (P(),) * 11
    return jax.shard_map(shards, mesh=mesh, in_specs=placed, out_specs=P("ia", "ja", None), check_vma=False)
```

```python
import jax
import jax.numpy as jnp
from jax import lax
from jax.experimental import pallas as pl
from jax.experimental.pallas import tpu as pltpu
from jax.sharding import PartitionSpec as P

BOTH = ("ia", "ja")
EPS = 1e-5
WIDE = 32
F32 = jnp.float32
BF16 = jnp.bfloat16
VMEM = pl.BlockSpec(memory_space=pltpu.VMEM)
SMEM = pl.BlockSpec(memory_space=pltpu.SMEM)


def device(xl, y, core, xh, z):
    return (((xl * 8 + y) * 2 + core) * 2 + xh) * 8 + z


def fold(half, m):
    return m if half == 0 else 7 - m


SHARING = [
    [device(xl, fold(half, m), core, xh, z) for xl in range(2) for m in range(4) for xh in range(2) for z in range(8)]
    for half in range(2)
    for core in range(2)
]
PLACES = [(xl, y, core, xh, z) for xl in range(2) for y in range(8) for core in range(2) for xh in range(2) for z in range(8)]
CORE_FLIP = [(device(xl, y, core, xh, z), device(xl, y, 1 - core, xh, z)) for xl, y, core, xh, z in PLACES]
HALF_FLIP = [(device(xl, y, core, xh, z), device(xl, 7 - y, core, xh, z)) for xl, y, core, xh, z in PLACES]


def sigmoid(x):
    return 1.0 / (1.0 + jnp.exp(-x))


def iota(shape, axis):
    return lax.broadcasted_iota(jnp.int32, shape, axis)


def contract(a, b, da, db):
    return lax.dot_general(a, b, (((da,), (db,)), ((), ())), preferred_element_type=F32)


def norm_kernel(place_ref, mask_ref, pair_ref, gain_ref, bias_ref, normed_ref, masked_ref):
    rows, cols, width = pair_ref.shape
    x = pair_ref[...].astype(F32).reshape(rows * cols, width)
    mean = jnp.mean(x, axis=-1, keepdims=True)
    centered = x - mean
    variance = jnp.mean(centered * centered, axis=-1, keepdims=True)
    normed = centered * lax.rsqrt(variance + EPS) * gain_ref[...] + bias_ref[...]
    normed_ref[...] = normed.astype(BF16)
    place = iota((cols, width), 0)
    col_valid = jnp.zeros((cols, width), F32)
    for k in range(cols):
        col_valid = jnp.where(place == k, mask_ref[place_ref[1] + k].astype(F32), col_valid)
    parts = []
    for i in [3 * ii + iq for iq in range(3) for ii in range(4)]:
        row_valid = mask_ref[place_ref[0] + i].astype(F32)
        parts.append(normed[i * cols : (i + 1) * cols] * (col_valid * row_valid))
        parts.append(jnp.zeros((WIDE - cols, width), F32))
    masked_ref[...] = jnp.concatenate(parts, axis=0).astype(BF16)


def edges_kernel(masked_ref, lg_ref, lv_ref, rg_ref, rv_ref, out_gain_ref, out_bias_ref, sent_ref, columns_ref, rows_ref):
    width = lg_ref.shape[0]
    columns_ref[0] = jnp.transpose(jnp.broadcast_to(out_gain_ref[...], (width, width)))
    columns_ref[1] = jnp.transpose(jnp.broadcast_to(out_bias_ref[...], (width, width)))
    masked = masked_ref[...]
    left = sigmoid(contract(lg_ref[...], masked, 0, 1)) * contract(lv_ref[...], masked, 0, 1)
    right = sigmoid(contract(rg_ref[...], masked, 0, 1)) * contract(rv_ref[...], masked, 0, 1)
    for t in range(3):
        lanes = slice(t * 128, (t + 1) * 128)
        rows_ref[t, pl.ds(0, width, stride=2), :] = right[:, lanes]
        rows_ref[t, pl.ds(1, width, stride=2), :] = left[:, lanes]
        sent_ref[:, :, lanes] = rows_ref[t].astype(BF16).reshape(width, 2, 128)


def swap_blocks(blocks, lane):
    out = []
    for b in range(4):
        total = None
        for a in range(4):
            moved = blocks[a] if a == b else pltpu.roll(blocks[a], (WIDE * (a - b)) % 128, blocks[a].ndim - 1)
            total = moved if total is None else jnp.where(lane // WIDE == a, moved, total)
        out.append(total)
    return out


def spread_side(side, got_ref, rows_ref, quads_ref):
    lane = iota((32, 128), 1)
    wide = iota((8, 128), 1) % WIDE < 24
    spread = {}
    for iq in range(3):
        rows_ref[iq] = got_ref[:, :, iq * 128 : (iq + 1) * 128].astype(F32).reshape(256, 128)
        blocks = [rows_ref[iq, pl.ds(2 * k + side, 32, stride=8), :] for k in range(4)]
        for ii, block in enumerate(swap_blocks(blocks, lane)):
            at = (iq * 4 + ii) * 32
            quads_ref[pl.ds(at, 32), :] = block
            found = [quads_ref[pl.ds(at + quad, 8, stride=4), :] for quad in range(4)]
            spread[iq, ii] = [jnp.where(wide, found[v], pltpu.roll(found[3], 24 - 8 * v, 1)) for v in range(3)]
    return spread


def right_kernel(got_ref, right_ref, rows_ref, quads_ref, padded_ref):
    padded_ref[...] = jnp.zeros_like(padded_ref)
    for (iq, ii), dense in spread_side(0, got_ref, rows_ref, quads_ref).items():
        for v in range(3):
            padded_ref[v, pl.ds(ii * 3 + iq, 8, stride=16), :] = dense[v]
    for v in range(3):
        right_ref[:, v * 128 : (v + 1) * 128] = padded_ref[v].astype(BF16)


def left_kernel(got_ref, left_ref, rows_ref, quads_ref):
    spread = spread_side(1, got_ref, rows_ref, quads_ref)
    for iq in range(3):
        for v in range(3):
            block = jnp.concatenate([spread[iq, ii][v] for ii in range(4)], axis=0)
            left_ref[iq * 32 : (iq + 1) * 32, v * 128 : (v + 1) * 128] = block.astype(BF16)


def mix_half(place_ref, other, left_ref, mine_ref, theirs_ref, sent_ref, slots_ref):
    lane = iota((8, 128), 1)
    left = left_ref[...]
    mine, theirs = mine_ref[...], theirs_ref[...]
    core = place_ref[2]
    half = place_ref[3 + other]
    first = jnp.where(core == 0, mine, theirs)
    second = jnp.where(core == 0, theirs, mine)
    for xl in range(2):
        pieces = []
        for m in range(4):
            at = (xl * 4 + m) * 16
            pieces += [first[at : at + 16], second[at : at + 16]]
        mixed = contract(left, jnp.concatenate(pieces, axis=0), 1, 1)
        high = mixed.astype(BF16).astype(F32)
        for iq in range(3):
            for part, values in enumerate((high, mixed - high)):
                blocks = [values[(iq * 4 + ii) * 8 : (iq * 4 + ii + 1) * 8] for ii in range(4)]
                for m, block in enumerate(swap_blocks(blocks, lane)):
                    slot = (m + half * (3 - 2 * m)) * 2 + part
                    slots_ref[xl * 3 + iq, pl.ds(pl.multiple_of(slot * 8, 8), 8), :] = block
            for g in range(8):
                rows = slots_ref[xl * 3 + iq, pl.ds(g, 8, stride=8), :]
                to = g * 16 + xl * 8 + half * 4
                sent_ref[pl.ds(to, 4), :, iq * 128 : (iq + 1) * 128] = rows.astype(BF16).reshape(4, 2, 128)


def near_kernel(
    place_ref,
    left_ref,
    mine_ref,
    theirs_ref,
    normed_ref,
    og_ref,
    sent_ref,
    gate_ref,
    slots_ref,
):
    mix_half(place_ref, 0, left_ref, mine_ref, theirs_ref, sent_ref, slots_ref)
    gate_ref[...] = sigmoid(contract(normed_ref[...], og_ref[...], 1, 0))


def far_kernel(place_ref, left_ref, mine_ref, theirs_ref, half_ref, sent_ref, slots_ref):
    del half_ref
    mix_half(place_ref, 1, left_ref, mine_ref, theirs_ref, sent_ref, slots_ref)


def update_kernel(got_ref, gate_ref, columns_ref, weight_ref, out_ref, rows_ref, flat_ref):
    rows, cols, width = out_ref.shape
    gain = columns_ref[0][:, 0:1]
    bias = columns_ref[1][:, 0:1]
    for iq in range(3):
        rows_ref[iq] = got_ref[:, :, iq * 128 : (iq + 1) * 128].astype(F32).reshape(2 * width, 128)
        mixed = rows_ref[iq, pl.ds(0, width, stride=2), :] + rows_ref[iq, pl.ds(1, width, stride=2), :]
        mean = jnp.mean(mixed, axis=0, keepdims=True)
        centered = mixed - mean
        variance = jnp.mean(centered * centered, axis=0, keepdims=True)
        normed = (centered * lax.rsqrt(variance + EPS) * gain + bias).astype(BF16)
        output = contract(normed, weight_ref[...], 0, 0)
        for ii in range(4):
            at = (3 * ii + iq) * cols
            flat_ref[at : at + 12, :] = output[ii * WIDE : ii * WIDE + 12]
            flat_ref[at + 12 : at + 24, :] = output[ii * WIDE + 16 : ii * WIDE + 28]
    out_ref[...] = (gate_ref[...] * flat_ref[...]).astype(BF16).reshape(rows, cols, width)


def shards(
    pair,
    token_mask,
    norm_in_gain,
    norm_in_bias,
    left_gate,
    left_value,
    right_gate,
    right_value,
    output_gate,
    norm_out_gain,
    norm_out_bias,
    output_weight,
):
    rows, cols, width = pair.shape
    params = pltpu.CompilerParams(vmem_limit_bytes=32 * 1024 * 1024)
    row_block = lax.axis_index("ia")
    half = row_block // 8 % 2
    place = jnp.stack([row_block * rows, lax.axis_index("ja") * cols, row_block % 2, half, 1 - half]).astype(jnp.int32)
    struct = jax.ShapeDtypeStruct
    normed, masked = pl.pallas_call(
        norm_kernel,
        name="norm",
        out_shape=(struct((rows * cols, width), BF16), struct((rows * WIDE, width), BF16)),
        in_specs=[SMEM, SMEM] + [VMEM] * 3,
        out_specs=(VMEM, VMEM),
        compiler_params=params,
    )(place, token_mask, pair, norm_in_gain.reshape(1, -1), norm_in_bias.reshape(1, -1))
    message = struct((128, 2, rows * WIDE), BF16)
    sent, columns = pl.pallas_call(
        edges_kernel,
        name="edges",
        out_shape=(message, struct((2, width, width), F32)),
        in_specs=[VMEM] * 7,
        out_specs=(VMEM, VMEM),
        scratch_shapes=[pltpu.VMEM((3, 256, 128), F32)],
        compiler_params=params,
    )(masked, left_gate, left_value, right_gate, right_value, norm_out_gain.reshape(1, -1), norm_out_bias.reshape(1, -1))
    got = lax.all_to_all(sent, BOTH, 0, 0, axis_index_groups=SHARING)
    scratch = [pltpu.VMEM((3, 256, 128), F32), pltpu.VMEM((384, 128), F32)]
    right = pl.pallas_call(
        right_kernel,
        name="right",
        out_shape=struct((128, 384), BF16),
        in_specs=[VMEM],
        out_specs=VMEM,
        scratch_shapes=scratch + [pltpu.VMEM((3, 128, 128), F32)],
        compiler_params=params,
    )(got)
    left = pl.pallas_call(
        left_kernel,
        name="left",
        out_shape=struct((96, 384), BF16),
        in_specs=[VMEM],
        out_specs=VMEM,
        scratch_shapes=scratch,
        compiler_params=params,
    )(got)
    near = lax.ppermute(right, BOTH, CORE_FLIP)
    far = lax.ppermute(right, BOTH, HALF_FLIP)
    both = lax.ppermute(far, BOTH, CORE_FLIP)
    sent, gate = pl.pallas_call(
        near_kernel,
        name="near",
        out_shape=(message, struct((rows * cols, width), F32)),
        in_specs=[SMEM] + [VMEM] * 5,
        out_specs=(VMEM, VMEM),
        scratch_shapes=[pltpu.VMEM((6, 64, 128), F32)],
        compiler_params=params,
    )(place, left, right, near, normed, output_gate)
    sent = pl.pallas_call(
        far_kernel,
        name="far",
        out_shape=message,
        in_specs=[SMEM] + [VMEM] * 4,
        out_specs=VMEM,
        scratch_shapes=[pltpu.VMEM((6, 64, 128), F32)],
        input_output_aliases={4: 0},
        compiler_params=params,
    )(place, left, far, both, sent)
    got = lax.all_to_all(sent, BOTH, 0, 0, axis_index_groups=SHARING)
    return pl.pallas_call(
        update_kernel,
        name="update",
        out_shape=struct((rows, cols, width), BF16),
        in_specs=[VMEM] * 4,
        out_specs=VMEM,
        scratch_shapes=[pltpu.VMEM((3, 256, 128), F32), pltpu.VMEM((rows * cols, 128), F32)],
        compiler_params=params,
    )(got, gate, columns, output_weight)


def solution(mesh):
    placed = (P("ia", "ja", None),) + (P(),) * 11
    return jax.shard_map(shards, mesh=mesh, in_specs=placed, out_specs=P("ia", "ja", None), check_vma=False)
```

```python
import jax
import jax.numpy as jnp
from jax import lax
from jax.experimental import pallas as pl
from jax.experimental.pallas import tpu as pltpu
from jax.sharding import PartitionSpec as P

BOTH = ("ia", "ja")
EPS = 1e-5
WIDE = 32
F32 = jnp.float32
BF16 = jnp.bfloat16
VMEM = pl.BlockSpec(memory_space=pltpu.VMEM)
SMEM = pl.BlockSpec(memory_space=pltpu.SMEM)


def device(xl, y, core, xh, z):
    return (((xl * 8 + y) * 2 + core) * 2 + xh) * 8 + z


def fold(half, m):
    return m if half == 0 else 7 - m


SHARING = [
    [device(xl, fold(half, m), core, xh, z) for xl in range(2) for m in range(4) for xh in range(2) for z in range(8)]
    for half in range(2)
    for core in range(2)
]
PLACES = [(xl, y, core, xh, z) for xl in range(2) for y in range(8) for core in range(2) for xh in range(2) for z in range(8)]
CORE_FLIP = [(device(xl, y, core, xh, z), device(xl, y, 1 - core, xh, z)) for xl, y, core, xh, z in PLACES]
HALF_FLIP = [(device(xl, y, core, xh, z), device(xl, 7 - y, core, xh, z)) for xl, y, core, xh, z in PLACES]


def sigmoid(x):
    return 1.0 / (1.0 + jnp.exp(-x))


def iota(shape, axis):
    return lax.broadcasted_iota(jnp.int32, shape, axis)


def contract(a, b, da, db):
    return lax.dot_general(a, b, (((da,), (db,)), ((), ())), preferred_element_type=F32)


def zeros_kernel(zeros_ref):
    zeros_ref[...] = jnp.zeros_like(zeros_ref)


def norm_kernel(place_ref, mask_ref, pair_ref, gain_ref, bias_ref, zeros_ref, normed_ref, masked_ref):
    rows, cols, width = pair_ref.shape
    x = pair_ref[...].astype(F32).reshape(rows * cols, width)
    mean = jnp.mean(x, axis=-1, keepdims=True)
    centered = x - mean
    variance = jnp.mean(centered * centered, axis=-1, keepdims=True)
    normed = centered * lax.rsqrt(variance + EPS) * gain_ref[...] + bias_ref[...]
    normed_ref[...] = normed.astype(BF16)
    place = iota((cols, width), 0)
    col_valid = jnp.zeros((cols, width), F32)
    for k in range(cols):
        col_valid = jnp.where(place == k, mask_ref[place_ref[1] + k].astype(F32), col_valid)
    parts = []
    for i in [3 * ii + iq for iq in range(3) for ii in range(4)]:
        row_valid = mask_ref[place_ref[0] + i].astype(F32)
        parts.append(normed[i * cols : (i + 1) * cols] * (col_valid * row_valid))
        parts.append(zeros_ref[0 : WIDE - cols])
    masked_ref[...] = jnp.concatenate(parts, axis=0).astype(BF16)


def edges_kernel(masked_ref, lg_ref, lv_ref, rg_ref, rv_ref, out_gain_ref, out_bias_ref, sent_ref, columns_ref, rows_ref):
    width = lg_ref.shape[0]
    columns_ref[0] = jnp.transpose(jnp.broadcast_to(out_gain_ref[...], (width, width)))
    columns_ref[1] = jnp.transpose(jnp.broadcast_to(out_bias_ref[...], (width, width)))
    masked = masked_ref[...]
    left = sigmoid(contract(lg_ref[...], masked, 0, 1)) * contract(lv_ref[...], masked, 0, 1)
    right = sigmoid(contract(rg_ref[...], masked, 0, 1)) * contract(rv_ref[...], masked, 0, 1)
    for t in range(3):
        lanes = slice(t * 128, (t + 1) * 128)
        rows_ref[t, pl.ds(0, width, stride=2), :] = right[:, lanes]
        rows_ref[t, pl.ds(1, width, stride=2), :] = left[:, lanes]
        sent_ref[:, :, lanes] = rows_ref[t].astype(BF16).reshape(width, 2, 128)


def swap_blocks(blocks, lane):
    out = []
    for b in range(4):
        total = None
        for a in range(4):
            moved = blocks[a] if a == b else pltpu.roll(blocks[a], (WIDE * (a - b)) % 128, blocks[a].ndim - 1)
            total = moved if total is None else jnp.where(lane // WIDE == a, moved, total)
        out.append(total)
    return out


def spread_side(side, got_ref, rows_ref, quads_ref):
    lane = iota((32, 128), 1)
    wide = iota((8, 128), 1) % WIDE < 24
    spread = {}
    for iq in range(3):
        rows_ref[iq] = got_ref[:, :, iq * 128 : (iq + 1) * 128].astype(F32).reshape(256, 128)
        blocks = [rows_ref[iq, pl.ds(2 * k + side, 32, stride=8), :] for k in range(4)]
        for ii, block in enumerate(swap_blocks(blocks, lane)):
            at = (iq * 4 + ii) * 32
            quads_ref[pl.ds(at, 32), :] = block
            found = [quads_ref[pl.ds(at + quad, 8, stride=4), :] for quad in range(4)]
            spread[iq, ii] = [jnp.where(wide, found[v], pltpu.roll(found[3], 24 - 8 * v, 1)) for v in range(3)]
    return spread


def right_kernel(got_ref, right_ref, rows_ref, quads_ref, dense_ref):
    for (iq, ii), dense in spread_side(0, got_ref, rows_ref, quads_ref).items():
        for v in range(3):
            dense_ref[v, pl.ds(ii * 3 + iq, 8, stride=12), :] = dense[v]
    for v in range(3):
        right_ref[:, v * 128 : (v + 1) * 128] = dense_ref[v].astype(BF16)


def left_kernel(got_ref, left_ref, rows_ref, quads_ref):
    spread = spread_side(1, got_ref, rows_ref, quads_ref)
    for iq in range(3):
        for v in range(3):
            block = jnp.concatenate([spread[iq, ii][v] for ii in range(4)], axis=0)
            left_ref[iq * 32 : (iq + 1) * 32, v * 128 : (v + 1) * 128] = block.astype(BF16)


def mix_half(place_ref, other, left_ref, mine_ref, theirs_ref, sent_ref, slots_ref):
    lane = iota((8, 128), 1)
    left = left_ref[...]
    core = place_ref[2]
    half = place_ref[3 + other]
    column = iota((96, 128), 0)
    side = jnp.where(column >= 48, 1, 0)
    m = sum(jnp.where(column - 48 * side >= 12 * n, 1, 0) for n in range(1, 4))
    to_lane = column - 48 * side + 20 * m + 16 * jnp.where(side == 0, core, 1 - core)
    spread = jnp.where(iota((96, 128), 1) == to_lane, 1.0, 0.0).astype(BF16)
    for xl in range(2):
        rows = slice(xl * 48, (xl + 1) * 48)
        right = jnp.concatenate([mine_ref[rows, :], theirs_ref[rows, :]], axis=0)
        mixed = contract(left, right, 1, 1)
        high = mixed.astype(BF16)
        low = (mixed - high.astype(F32)).astype(BF16)
        high, low = contract(high, spread, 1, 0), contract(low, spread, 1, 0)
        for iq in range(3):
            for part, values in enumerate((high, low)):
                blocks = [values[(iq * 4 + ii) * 8 : (iq * 4 + ii + 1) * 8] for ii in range(4)]
                for m, block in enumerate(swap_blocks(blocks, lane)):
                    slot = (m + half * (3 - 2 * m)) * 2 + part
                    slots_ref[xl * 3 + iq, pl.ds(pl.multiple_of(slot * 8, 8), 8), :] = block
            for g in range(8):
                rows = slots_ref[xl * 3 + iq, pl.ds(g, 8, stride=8), :]
                to = g * 16 + xl * 8 + half * 4
                sent_ref[pl.ds(to, 4), :, iq * 128 : (iq + 1) * 128] = rows.astype(BF16).reshape(4, 2, 128)


def near_kernel(
    place_ref,
    left_ref,
    mine_ref,
    theirs_ref,
    normed_ref,
    og_ref,
    sent_ref,
    gate_ref,
    slots_ref,
):
    mix_half(place_ref, 0, left_ref, mine_ref, theirs_ref, sent_ref, slots_ref)
    gate_ref[...] = sigmoid(contract(normed_ref[...], og_ref[...], 1, 0))


def far_kernel(place_ref, left_ref, mine_ref, theirs_ref, half_ref, sent_ref, slots_ref):
    del half_ref
    mix_half(place_ref, 1, left_ref, mine_ref, theirs_ref, sent_ref, slots_ref)


def update_kernel(got_ref, gate_ref, columns_ref, weight_ref, out_ref, rows_ref, flat_ref):
    rows, cols, width = out_ref.shape
    gain = columns_ref[0][:, 0:1]
    bias = columns_ref[1][:, 0:1]
    for iq in range(3):
        rows_ref[iq] = got_ref[:, :, iq * 128 : (iq + 1) * 128].astype(F32).reshape(2 * width, 128)
        mixed = rows_ref[iq, pl.ds(0, width, stride=2), :] + rows_ref[iq, pl.ds(1, width, stride=2), :]
        mean = jnp.mean(mixed, axis=0, keepdims=True)
        centered = mixed - mean
        variance = jnp.mean(centered * centered, axis=0, keepdims=True)
        normed = (centered * lax.rsqrt(variance + EPS) * gain + bias).astype(BF16)
        output = contract(normed, weight_ref[...], 0, 0)
        for ii in range(4):
            at = (3 * ii + iq) * cols
            flat_ref[at : at + 12, :] = output[ii * WIDE : ii * WIDE + 12]
            flat_ref[at + 12 : at + 24, :] = output[ii * WIDE + 16 : ii * WIDE + 28]
    out_ref[...] = (gate_ref[...] * flat_ref[...]).astype(BF16).reshape(rows, cols, width)


def shards(
    pair,
    token_mask,
    norm_in_gain,
    norm_in_bias,
    left_gate,
    left_value,
    right_gate,
    right_value,
    output_gate,
    norm_out_gain,
    norm_out_bias,
    output_weight,
):
    rows, cols, width = pair.shape
    params = pltpu.CompilerParams(vmem_limit_bytes=32 * 1024 * 1024)
    row_block = lax.axis_index("ia")
    half = row_block // 8 % 2
    place = jnp.stack([row_block * rows, lax.axis_index("ja") * cols, row_block % 2, half, 1 - half]).astype(jnp.int32)
    struct = jax.ShapeDtypeStruct
    zeros = pl.pallas_call(
        zeros_kernel,
        name="zeros",
        out_shape=struct((width, width), F32),
        out_specs=VMEM,
        compiler_params=params,
    )()
    normed, masked = pl.pallas_call(
        norm_kernel,
        name="norm",
        out_shape=(struct((rows * cols, width), BF16), struct((rows * WIDE, width), BF16)),
        in_specs=[SMEM, SMEM] + [VMEM] * 4,
        out_specs=(VMEM, VMEM),
        compiler_params=params,
    )(place, token_mask, pair, norm_in_gain.reshape(1, -1), norm_in_bias.reshape(1, -1), zeros)
    message = struct((128, 2, rows * WIDE), BF16)
    sent, columns = pl.pallas_call(
        edges_kernel,
        name="edges",
        out_shape=(message, struct((2, width, width), F32)),
        in_specs=[VMEM] * 7,
        out_specs=(VMEM, VMEM),
        scratch_shapes=[pltpu.VMEM((3, 256, 128), F32)],
        compiler_params=params,
    )(masked, left_gate, left_value, right_gate, right_value, norm_out_gain.reshape(1, -1), norm_out_bias.reshape(1, -1))
    got = lax.all_to_all(sent, BOTH, 0, 0, axis_index_groups=SHARING)
    scratch = [pltpu.VMEM((3, 256, 128), F32), pltpu.VMEM((384, 128), F32)]
    right = pl.pallas_call(
        right_kernel,
        name="right",
        out_shape=struct((96, 384), BF16),
        in_specs=[VMEM],
        out_specs=VMEM,
        scratch_shapes=scratch + [pltpu.VMEM((3, 96, 128), F32)],
        compiler_params=params,
    )(got)
    left = pl.pallas_call(
        left_kernel,
        name="left",
        out_shape=struct((96, 384), BF16),
        in_specs=[VMEM],
        out_specs=VMEM,
        scratch_shapes=scratch,
        compiler_params=params,
    )(got)
    near = lax.ppermute(right, BOTH, CORE_FLIP)
    far = lax.ppermute(right, BOTH, HALF_FLIP)
    both = lax.ppermute(far, BOTH, CORE_FLIP)
    sent, gate = pl.pallas_call(
        near_kernel,
        name="near",
        out_shape=(message, struct((rows * cols, width), F32)),
        in_specs=[SMEM] + [VMEM] * 5,
        out_specs=(VMEM, VMEM),
        scratch_shapes=[pltpu.VMEM((6, 64, 128), F32)],
        compiler_params=params,
    )(place, left, right, near, normed, output_gate)
    sent = pl.pallas_call(
        far_kernel,
        name="far",
        out_shape=message,
        in_specs=[SMEM] + [VMEM] * 4,
        out_specs=VMEM,
        scratch_shapes=[pltpu.VMEM((6, 64, 128), F32)],
        input_output_aliases={4: 0},
        compiler_params=params,
    )(place, left, far, both, sent)
    got = lax.all_to_all(sent, BOTH, 0, 0, axis_index_groups=SHARING)
    return pl.pallas_call(
        update_kernel,
        name="update",
        out_shape=struct((rows, cols, width), BF16),
        in_specs=[VMEM] * 4,
        out_specs=VMEM,
        scratch_shapes=[pltpu.VMEM((3, 256, 128), F32), pltpu.VMEM((rows * cols, 128), F32)],
        compiler_params=params,
    )(got, gate, columns, output_weight)


def solution(mesh):
    placed = (P("ia", "ja", None),) + (P(),) * 11
    return jax.shard_map(shards, mesh=mesh, in_specs=placed, out_specs=P("ia", "ja", None), check_vma=False)
```

```python
import jax
import jax.numpy as jnp
from jax import lax
from jax.experimental import pallas as pl
from jax.experimental.pallas import tpu as pltpu
from jax.sharding import PartitionSpec as P

BOTH = ("ia", "ja")
EPS = 1e-5
WIDE = 32
F32 = jnp.float32
BF16 = jnp.bfloat16
VMEM = pl.BlockSpec(memory_space=pltpu.VMEM)
SMEM = pl.BlockSpec(memory_space=pltpu.SMEM)


def device(xl, y, core, xh, z):
    return (((xl * 8 + y) * 2 + core) * 2 + xh) * 8 + z


def fold(half, m):
    return m if half == 0 else 7 - m


SHARING = [
    [device(xl, fold(half, m), core, xh, z) for xl in range(2) for m in range(4) for xh in range(2) for z in range(8)]
    for half in range(2)
    for core in range(2)
]
PLACES = [(xl, y, core, xh, z) for xl in range(2) for y in range(8) for core in range(2) for xh in range(2) for z in range(8)]
CORE_FLIP = [(device(xl, y, core, xh, z), device(xl, y, 1 - core, xh, z)) for xl, y, core, xh, z in PLACES]
HALF_FLIP = [(device(xl, y, core, xh, z), device(xl, 7 - y, core, xh, z)) for xl, y, core, xh, z in PLACES]


def sigmoid(x):
    return 1.0 / (1.0 + jnp.exp(-x))


def iota(shape, axis):
    return lax.broadcasted_iota(jnp.int32, shape, axis)


def contract(a, b, da, db):
    return lax.dot_general(a, b, (((da,), (db,)), ((), ())), preferred_element_type=F32)


def first_kernel(place_ref, zeros_ref, spread_ref):
    zeros_ref[...] = jnp.zeros_like(zeros_ref)
    row = iota(spread_ref.shape, 0)
    side = jnp.where(row >= 96, 1, 0)
    row = row - 96 * side
    run = sum(jnp.where(row >= 12 * n, 1, 0) for n in range(1, 8))
    core = place_ref[2]
    to_lane = row + 20 * run + 16 * jnp.where(side == 0, core, 1 - core)
    spread_ref[...] = jnp.where(iota(spread_ref.shape, 1) == to_lane, 1.0, 0.0).astype(BF16)


def norm_kernel(
    place_ref,
    mask_ref,
    pair_ref,
    gain_ref,
    bias_ref,
    out_gain_ref,
    out_bias_ref,
    zeros_ref,
    normed_ref,
    masked_ref,
    columns_ref,
):
    rows, cols, width = pair_ref.shape
    x = pair_ref[...].astype(F32).reshape(rows * cols, width)
    mean = jnp.mean(x, axis=-1, keepdims=True)
    centered = x - mean
    variance = jnp.mean(centered * centered, axis=-1, keepdims=True)
    normed = centered * lax.rsqrt(variance + EPS) * gain_ref[...] + bias_ref[...]
    normed_ref[...] = normed.astype(BF16)
    columns_ref[0] = jnp.transpose(jnp.broadcast_to(out_gain_ref[...], (width, width)))
    columns_ref[1] = jnp.transpose(jnp.broadcast_to(out_bias_ref[...], (width, width)))
    place = iota((cols, width), 0)
    col_valid = jnp.zeros((cols, width), F32)
    for k in range(cols):
        col_valid = jnp.where(place == k, mask_ref[place_ref[1] + k].astype(F32), col_valid)
    parts = []
    for i in [3 * ii + iq for iq in range(3) for ii in range(4)]:
        row_valid = mask_ref[place_ref[0] + i].astype(F32)
        parts.append(normed[i * cols : (i + 1) * cols] * (col_valid * row_valid))
        parts.append(zeros_ref[0 : WIDE - cols])
    masked_ref[...] = jnp.concatenate(parts, axis=0).astype(BF16)


def edges_kernel(masked_ref, lg_ref, lv_ref, rg_ref, rv_ref, sent_ref, rows_ref):
    width = lg_ref.shape[0]
    masked = masked_ref[...]
    left = sigmoid(contract(lg_ref[...], masked, 0, 1)) * contract(lv_ref[...], masked, 0, 1)
    right = sigmoid(contract(rg_ref[...], masked, 0, 1)) * contract(rv_ref[...], masked, 0, 1)
    for t in range(3):
        lanes = slice(t * 128, (t + 1) * 128)
        rows_ref[t, pl.ds(0, width, stride=2), :] = right[:, lanes]
        rows_ref[t, pl.ds(1, width, stride=2), :] = left[:, lanes]
        sent_ref[:, :, lanes] = rows_ref[t].astype(BF16).reshape(width, 2, 128)


def swap_blocks(blocks, lane):
    out = []
    for b in range(4):
        total = None
        for a in range(4):
            moved = blocks[a] if a == b else pltpu.roll(blocks[a], (WIDE * (a - b)) % 128, blocks[a].ndim - 1)
            total = moved if total is None else jnp.where(lane // WIDE == a, moved, total)
        out.append(total)
    return out


def spread_side(side, got_ref, rows_ref, quads_ref):
    lane = iota((32, 128), 1)
    wide = iota((8, 128), 1) % WIDE < 24
    spread = {}
    for iq in range(3):
        rows_ref[iq] = got_ref[:, :, iq * 128 : (iq + 1) * 128].astype(F32).reshape(256, 128)
        blocks = [rows_ref[iq, pl.ds(2 * k + side, 32, stride=8), :] for k in range(4)]
        for ii, block in enumerate(swap_blocks(blocks, lane)):
            at = (iq * 4 + ii) * 32
            quads_ref[pl.ds(at, 32), :] = block
            found = [quads_ref[pl.ds(at + quad, 8, stride=4), :] for quad in range(4)]
            spread[iq, ii] = [jnp.where(wide, found[v], pltpu.roll(found[3], 24 - 8 * v, 1)) for v in range(3)]
    return spread


def right_kernel(got_ref, right_ref, rows_ref, quads_ref, dense_ref):
    for (iq, ii), dense in spread_side(0, got_ref, rows_ref, quads_ref).items():
        for v in range(3):
            dense_ref[v, pl.ds(ii * 3 + iq, 8, stride=12), :] = dense[v]
    for v in range(3):
        right_ref[:, v * 128 : (v + 1) * 128] = dense_ref[v].astype(BF16)


def left_kernel(got_ref, left_ref, rows_ref, quads_ref):
    spread = spread_side(1, got_ref, rows_ref, quads_ref)
    for iq in range(3):
        for v in range(3):
            block = jnp.concatenate([spread[iq, ii][v] for ii in range(4)], axis=0)
            left_ref[iq * 32 : (iq + 1) * 32, v * 128 : (v + 1) * 128] = block.astype(BF16)


def mix_half(place_ref, other, left_ref, mine_ref, theirs_ref, spread_ref, sent_ref, slots_ref):
    lane = iota((8, 128), 1)
    half = place_ref[3 + other]
    mixed = contract(left_ref[...], jnp.concatenate([mine_ref[...], theirs_ref[...]], axis=0), 1, 1)
    high = mixed.astype(BF16)
    low = (mixed - high.astype(F32)).astype(BF16)
    parts = contract(jnp.concatenate([high, low], axis=0), spread_ref[...], 1, 0)
    for xl in range(2):
        for iq in range(3):
            for part in range(2):
                at = part * 96 + iq * 32
                blocks = [parts[at + ii * 8 : at + (ii + 1) * 8, xl * 128 : (xl + 1) * 128] for ii in range(4)]
                for m, block in enumerate(swap_blocks(blocks, lane)):
                    slot = (m + half * (3 - 2 * m)) * 2 + part
                    slots_ref[xl * 3 + iq, pl.ds(pl.multiple_of(slot * 8, 8), 8), :] = block
            for g in range(8):
                rows = slots_ref[xl * 3 + iq, pl.ds(g, 8, stride=8), :]
                to = g * 16 + xl * 8 + half * 4
                sent_ref[pl.ds(to, 4), :, iq * 128 : (iq + 1) * 128] = rows.astype(BF16).reshape(4, 2, 128)


def near_kernel(
    place_ref,
    left_ref,
    mine_ref,
    theirs_ref,
    spread_ref,
    normed_ref,
    og_ref,
    sent_ref,
    gate_ref,
    slots_ref,
):
    mix_half(place_ref, 0, left_ref, mine_ref, theirs_ref, spread_ref, sent_ref, slots_ref)
    gate_ref[...] = sigmoid(contract(normed_ref[...], og_ref[...], 1, 0))


def far_kernel(place_ref, left_ref, mine_ref, theirs_ref, spread_ref, half_ref, sent_ref, slots_ref):
    del half_ref
    mix_half(place_ref, 1, left_ref, mine_ref, theirs_ref, spread_ref, sent_ref, slots_ref)


def update_kernel(got_ref, gate_ref, columns_ref, weight_ref, out_ref, rows_ref, flat_ref):
    rows, cols, width = out_ref.shape
    gain = columns_ref[0][:, 0:1]
    bias = columns_ref[1][:, 0:1]
    for iq in range(3):
        rows_ref[iq] = got_ref[:, :, iq * 128 : (iq + 1) * 128].astype(F32).reshape(2 * width, 128)
        mixed = rows_ref[iq, pl.ds(0, width, stride=2), :] + rows_ref[iq, pl.ds(1, width, stride=2), :]
        mean = jnp.mean(mixed, axis=0, keepdims=True)
        centered = mixed - mean
        variance = jnp.mean(centered * centered, axis=0, keepdims=True)
        normed = (centered * lax.rsqrt(variance + EPS) * gain + bias).astype(BF16)
        output = contract(normed, weight_ref[...], 0, 0)
        for ii in range(4):
            at = (3 * ii + iq) * cols
            flat_ref[at : at + 12, :] = output[ii * WIDE : ii * WIDE + 12]
            flat_ref[at + 12 : at + 24, :] = output[ii * WIDE + 16 : ii * WIDE + 28]
    out_ref[...] = (gate_ref[...] * flat_ref[...]).astype(BF16).reshape(rows, cols, width)


def shards(
    pair,
    token_mask,
    norm_in_gain,
    norm_in_bias,
    left_gate,
    left_value,
    right_gate,
    right_value,
    output_gate,
    norm_out_gain,
    norm_out_bias,
    output_weight,
):
    rows, cols, width = pair.shape
    params = pltpu.CompilerParams(vmem_limit_bytes=32 * 1024 * 1024)
    row_block = lax.axis_index("ia")
    half = row_block // 8 % 2
    place = jnp.stack([row_block * rows, lax.axis_index("ja") * cols, row_block % 2, half, 1 - half]).astype(jnp.int32)
    struct = jax.ShapeDtypeStruct
    zeros, spread = pl.pallas_call(
        first_kernel,
        name="first",
        out_shape=(struct((width, width), F32), struct((192, 256), BF16)),
        in_specs=[SMEM],
        out_specs=(VMEM, VMEM),
        compiler_params=params,
    )(place)
    normed, masked, columns = pl.pallas_call(
        norm_kernel,
        name="norm",
        out_shape=(
            struct((rows * cols, width), BF16),
            struct((rows * WIDE, width), BF16),
            struct((2, width, width), F32),
        ),
        in_specs=[SMEM, SMEM] + [VMEM] * 6,
        out_specs=(VMEM, VMEM, VMEM),
        compiler_params=params,
    )(
        place,
        token_mask,
        pair,
        norm_in_gain.reshape(1, -1),
        norm_in_bias.reshape(1, -1),
        norm_out_gain.reshape(1, -1),
        norm_out_bias.reshape(1, -1),
        zeros,
    )
    message = struct((128, 2, rows * WIDE), BF16)
    sent = pl.pallas_call(
        edges_kernel,
        name="edges",
        out_shape=message,
        in_specs=[VMEM] * 5,
        out_specs=VMEM,
        scratch_shapes=[pltpu.VMEM((3, 256, 128), F32)],
        compiler_params=params,
    )(masked, left_gate, left_value, right_gate, right_value)
    got = lax.all_to_all(sent, BOTH, 0, 0, axis_index_groups=SHARING)
    scratch = [pltpu.VMEM((3, 256, 128), F32), pltpu.VMEM((384, 128), F32)]
    right = pl.pallas_call(
        right_kernel,
        name="right",
        out_shape=struct((96, 384), BF16),
        in_specs=[VMEM],
        out_specs=VMEM,
        scratch_shapes=scratch + [pltpu.VMEM((3, 96, 128), F32)],
        compiler_params=params,
    )(got)
    left = pl.pallas_call(
        left_kernel,
        name="left",
        out_shape=struct((96, 384), BF16),
        in_specs=[VMEM],
        out_specs=VMEM,
        scratch_shapes=scratch,
        compiler_params=params,
    )(got)
    near = lax.ppermute(right, BOTH, CORE_FLIP)
    far = lax.ppermute(right, BOTH, HALF_FLIP)
    both = lax.ppermute(far, BOTH, CORE_FLIP)
    sent, gate = pl.pallas_call(
        near_kernel,
        name="near",
        out_shape=(message, struct((rows * cols, width), F32)),
        in_specs=[SMEM] + [VMEM] * 6,
        out_specs=(VMEM, VMEM),
        scratch_shapes=[pltpu.VMEM((6, 64, 128), F32)],
        compiler_params=params,
    )(place, left, right, near, spread, normed, output_gate)
    sent = pl.pallas_call(
        far_kernel,
        name="far",
        out_shape=message,
        in_specs=[SMEM] + [VMEM] * 5,
        out_specs=VMEM,
        scratch_shapes=[pltpu.VMEM((6, 64, 128), F32)],
        input_output_aliases={5: 0},
        compiler_params=params,
    )(place, left, far, both, spread, sent)
    got = lax.all_to_all(sent, BOTH, 0, 0, axis_index_groups=SHARING)
    return pl.pallas_call(
        update_kernel,
        name="update",
        out_shape=struct((rows, cols, width), BF16),
        in_specs=[VMEM] * 4,
        out_specs=VMEM,
        scratch_shapes=[pltpu.VMEM((3, 256, 128), F32), pltpu.VMEM((rows * cols, 128), F32)],
        compiler_params=params,
    )(got, gate, columns, output_weight)


def solution(mesh):
    placed = (P("ia", "ja", None),) + (P(),) * 11
    return jax.shard_map(shards, mesh=mesh, in_specs=placed, out_specs=P("ia", "ja", None), check_vma=False)
```

```python
import jax
import jax.numpy as jnp
from jax import lax
from jax.experimental import pallas as pl
from jax.experimental.pallas import tpu as pltpu
from jax.sharding import PartitionSpec as P

BOTH = ("ia", "ja")
EPS = 1e-5
WIDE = 32
F32 = jnp.float32
BF16 = jnp.bfloat16
VMEM = pl.BlockSpec(memory_space=pltpu.VMEM)
SMEM = pl.BlockSpec(memory_space=pltpu.SMEM)
HBM = pl.BlockSpec(memory_space=pltpu.HBM)


def device(xl, y, core, xh, z):
    return (((xl * 8 + y) * 2 + core) * 2 + xh) * 8 + z


def fold(half, m):
    return m if half == 0 else 7 - m


SHARING = [
    [device(xl, fold(half, m), core, xh, z) for xl in range(2) for m in range(4) for xh in range(2) for z in range(8)]
    for half in range(2)
    for core in range(2)
]
PLACES = [(xl, y, core, xh, z) for xl in range(2) for y in range(8) for core in range(2) for xh in range(2) for z in range(8)]
CORE_FLIP = [(device(xl, y, core, xh, z), device(xl, y, 1 - core, xh, z)) for xl, y, core, xh, z in PLACES]
HALF_FLIP = [(device(xl, y, core, xh, z), device(xl, 7 - y, core, xh, z)) for xl, y, core, xh, z in PLACES]


def sigmoid(x):
    return 1.0 / (1.0 + jnp.exp(-x))


def iota(shape, axis):
    return lax.broadcasted_iota(jnp.int32, shape, axis)


def contract(a, b, da, db):
    return lax.dot_general(a, b, (((da,), (db,)), ((), ())), preferred_element_type=F32)


def edges_kernel(
    place_ref,
    pair_hbm,
    mask_hbm,
    gain_hbm,
    bias_hbm,
    out_gain_hbm,
    out_bias_hbm,
    lg_hbm,
    lv_hbm,
    rg_hbm,
    rv_hbm,
    sent_ref,
    normed_ref,
    columns_ref,
    spread_ref,
    pair_ref,
    mask_ref,
    gain_ref,
    bias_ref,
    out_gain_ref,
    out_bias_ref,
    lg_ref,
    lv_ref,
    rg_ref,
    rv_ref,
    rows_ref,
    arrived,
):
    fetches = [
        (pair_hbm, pair_ref),
        (mask_hbm, mask_ref),
        (gain_hbm, gain_ref),
        (bias_hbm, bias_ref),
        (lg_hbm, lg_ref),
        (lv_hbm, lv_ref),
        (rg_hbm, rg_ref),
        (rv_hbm, rv_ref),
        (out_gain_hbm, out_gain_ref),
        (out_bias_hbm, out_bias_ref),
    ]
    copies = [pltpu.make_async_copy(source, to, arrived.at[n]) for n, (source, to) in enumerate(fetches)]
    for copy in copies:
        copy.start()
    row = iota(spread_ref.shape, 0)
    side = jnp.where(row >= 96, 1, 0)
    row = row - 96 * side
    run = sum(jnp.where(row >= 12 * n, 1, 0) for n in range(1, 8))
    core = place_ref[2]
    to_lane = row + 20 * run + 16 * jnp.where(side == 0, core, 1 - core)
    spread_ref[...] = jnp.where(iota(spread_ref.shape, 1) == to_lane, 1.0, 0.0).astype(BF16)
    for copy in copies[:4]:
        copy.wait()
    width = lg_ref.shape[0]
    rows, cols = 12, 24
    x = pair_ref[...].astype(F32)
    mean = jnp.mean(x, axis=-1, keepdims=True)
    centered = x - mean
    variance = jnp.mean(centered * centered, axis=-1, keepdims=True)
    normed = centered * lax.rsqrt(variance + EPS) * gain_ref[...] + bias_ref[...]
    normed_ref[...] = normed.astype(BF16)
    place = iota((cols, width), 0)
    col_valid = jnp.zeros((cols, width), F32)
    for k in range(cols):
        col_valid = jnp.where(place == k, mask_ref[place_ref[1] + k].astype(F32), col_valid)
    parts = []
    for i in [3 * ii + iq for iq in range(3) for ii in range(4)]:
        row_valid = mask_ref[place_ref[0] + i].astype(F32)
        parts.append(normed[i * cols : (i + 1) * cols] * (col_valid * row_valid))
        parts.append(jnp.zeros((WIDE - cols, width), F32))
    masked = jnp.concatenate(parts, axis=0).astype(BF16)
    for copy in copies[4:]:
        copy.wait()
    left = sigmoid(contract(lg_ref[...], masked, 0, 1)) * contract(lv_ref[...], masked, 0, 1)
    right = sigmoid(contract(rg_ref[...], masked, 0, 1)) * contract(rv_ref[...], masked, 0, 1)
    for t in range(3):
        lanes = slice(t * 128, (t + 1) * 128)
        rows_ref[t, pl.ds(0, width, stride=2), :] = right[:, lanes]
        rows_ref[t, pl.ds(1, width, stride=2), :] = left[:, lanes]
        sent_ref[:, :, lanes] = rows_ref[t].astype(BF16).reshape(width, 2, 128)
    columns_ref[0] = jnp.transpose(jnp.broadcast_to(out_gain_ref[...], (width, width)))
    columns_ref[1] = jnp.transpose(jnp.broadcast_to(out_bias_ref[...], (width, width)))


def swap_blocks(blocks, lane):
    out = []
    for b in range(4):
        total = None
        for a in range(4):
            moved = blocks[a] if a == b else pltpu.roll(blocks[a], (WIDE * (a - b)) % 128, blocks[a].ndim - 1)
            total = moved if total is None else jnp.where(lane // WIDE == a, moved, total)
        out.append(total)
    return out


def spread_side(side, got_ref, rows_ref, quads_ref):
    lane = iota((32, 128), 1)
    wide = iota((8, 128), 1) % WIDE < 24
    spread = {}
    for iq in range(3):
        rows_ref[iq] = got_ref[:, :, iq * 128 : (iq + 1) * 128].astype(F32).reshape(256, 128)
        blocks = [rows_ref[iq, pl.ds(2 * k + side, 32, stride=8), :] for k in range(4)]
        for ii, block in enumerate(swap_blocks(blocks, lane)):
            at = (iq * 4 + ii) * 32
            quads_ref[pl.ds(at, 32), :] = block
            found = [quads_ref[pl.ds(at + quad, 8, stride=4), :] for quad in range(4)]
            spread[iq, ii] = [jnp.where(wide, found[v], pltpu.roll(found[3], 24 - 8 * v, 1)) for v in range(3)]
    return spread


def right_kernel(got_ref, right_ref, rows_ref, quads_ref, dense_ref):
    for (iq, ii), dense in spread_side(0, got_ref, rows_ref, quads_ref).items():
        for v in range(3):
            dense_ref[v, pl.ds(ii * 3 + iq, 8, stride=12), :] = dense[v]
    for v in range(3):
        right_ref[:, v * 128 : (v + 1) * 128] = dense_ref[v].astype(BF16)


def mix_half(place_ref, other, left_ref, mine_ref, theirs_ref, spread_ref, sent_ref, slots_ref):
    lane = iota((8, 128), 1)
    half = place_ref[3 + other]
    mixed = contract(left_ref[...], jnp.concatenate([mine_ref[...], theirs_ref[...]], axis=0), 1, 1)
    high = mixed.astype(BF16)
    low = (mixed - high.astype(F32)).astype(BF16)
    parts = contract(jnp.concatenate([high, low], axis=0), spread_ref[...], 1, 0)
    for xl in range(2):
        for iq in range(3):
            for part in range(2):
                at = part * 96 + iq * 32
                blocks = [parts[at + ii * 8 : at + (ii + 1) * 8, xl * 128 : (xl + 1) * 128] for ii in range(4)]
                for m, block in enumerate(swap_blocks(blocks, lane)):
                    slot = (m + half * (3 - 2 * m)) * 2 + part
                    slots_ref[xl * 3 + iq, pl.ds(pl.multiple_of(slot * 8, 8), 8), :] = block
            for g in range(8):
                rows = slots_ref[xl * 3 + iq, pl.ds(g, 8, stride=8), :]
                to = g * 16 + xl * 8 + half * 4
                sent_ref[pl.ds(to, 4), :, iq * 128 : (iq + 1) * 128] = rows.astype(BF16).reshape(4, 2, 128)


def near_kernel(
    place_ref,
    got_ref,
    mine_ref,
    theirs_ref,
    spread_ref,
    normed_ref,
    og_ref,
    sent_ref,
    gate_ref,
    left_ref,
    slots_ref,
    rows_ref,
    quads_ref,
):
    blocks = spread_side(1, got_ref, rows_ref, quads_ref)
    for iq in range(3):
        for v in range(3):
            block = jnp.concatenate([blocks[iq, ii][v] for ii in range(4)], axis=0)
            left_ref[iq * 32 : (iq + 1) * 32, v * 128 : (v + 1) * 128] = block.astype(BF16)
    gate_ref[...] = sigmoid(contract(normed_ref[...], og_ref[...], 1, 0))
    mix_half(place_ref, 0, left_ref, mine_ref, theirs_ref, spread_ref, sent_ref, slots_ref)


def far_kernel(place_ref, left_ref, mine_ref, theirs_ref, spread_ref, half_ref, sent_ref, slots_ref):
    del half_ref
    mix_half(place_ref, 1, left_ref, mine_ref, theirs_ref, spread_ref, sent_ref, slots_ref)


def update_kernel(got_ref, gate_ref, columns_ref, weight_ref, out_ref, rows_ref, flat_ref):
    rows, cols, width = out_ref.shape
    gain = columns_ref[0][:, 0:1]
    bias = columns_ref[1][:, 0:1]
    for iq in range(3):
        rows_ref[iq] = got_ref[:, :, iq * 128 : (iq + 1) * 128].astype(F32).reshape(2 * width, 128)
        mixed = rows_ref[iq, pl.ds(0, width, stride=2), :] + rows_ref[iq, pl.ds(1, width, stride=2), :]
        mean = jnp.mean(mixed, axis=0, keepdims=True)
        centered = mixed - mean
        variance = jnp.mean(centered * centered, axis=0, keepdims=True)
        normed = (centered * lax.rsqrt(variance + EPS) * gain + bias).astype(BF16)
        output = contract(normed, weight_ref[...], 0, 0)
        for ii in range(4):
            at = (3 * ii + iq) * cols
            flat_ref[at : at + 12, :] = output[ii * WIDE : ii * WIDE + 12]
            flat_ref[at + 12 : at + 24, :] = output[ii * WIDE + 16 : ii * WIDE + 28]
    out_ref[...] = (gate_ref[...] * flat_ref[...]).astype(BF16).reshape(rows, cols, width)


def shards(
    pair,
    token_mask,
    norm_in_gain,
    norm_in_bias,
    left_gate,
    left_value,
    right_gate,
    right_value,
    output_gate,
    norm_out_gain,
    norm_out_bias,
    output_weight,
):
    rows, cols, width = pair.shape
    params = pltpu.CompilerParams(vmem_limit_bytes=32 * 1024 * 1024)
    row_block = lax.axis_index("ia")
    half = row_block // 8 % 2
    place = jnp.stack([row_block * rows, lax.axis_index("ja") * cols, row_block % 2, half, 1 - half]).astype(jnp.int32)
    struct = jax.ShapeDtypeStruct
    message = struct((width, 2, rows * WIDE), BF16)
    arrays = [pair.reshape(rows * cols, width), token_mask]
    arrays += [v.reshape(1, -1) for v in (norm_in_gain, norm_in_bias, norm_out_gain, norm_out_bias)]
    arrays += [left_gate, left_value, right_gate, right_value]
    fetched = [pltpu.VMEM(array.shape, array.dtype) for array in arrays]
    fetched[1] = pltpu.SMEM(token_mask.shape, token_mask.dtype)
    sent, normed, columns, spread = pl.pallas_call(
        edges_kernel,
        name="edges",
        out_shape=(
            message,
            struct((rows * cols, width), BF16),
            struct((2, width, width), F32),
            struct((192, 256), BF16),
        ),
        in_specs=[SMEM] + [HBM] * 10,
        out_specs=(VMEM,) * 4,
        scratch_shapes=fetched + [pltpu.VMEM((3, 256, 128), F32), pltpu.SemaphoreType.DMA((10,))],
        compiler_params=params,
    )(place, *[pltpu.with_memory_space_constraint(array, pltpu.HBM) for array in arrays])
    got = lax.all_to_all(sent, BOTH, 0, 0, axis_index_groups=SHARING)
    scratch = [pltpu.VMEM((3, 256, 128), F32), pltpu.VMEM((384, 128), F32)]
    right = pl.pallas_call(
        right_kernel,
        name="right",
        out_shape=struct((96, 384), BF16),
        in_specs=[VMEM],
        out_specs=VMEM,
        scratch_shapes=scratch + [pltpu.VMEM((3, 96, 128), F32)],
        compiler_params=params,
    )(got)
    near = lax.ppermute(right, BOTH, CORE_FLIP)
    far = lax.ppermute(right, BOTH, HALF_FLIP)
    both = lax.ppermute(far, BOTH, CORE_FLIP)
    sent, gate, left = pl.pallas_call(
        near_kernel,
        name="near",
        out_shape=(message, struct((rows * cols, width), F32), struct((96, 384), BF16)),
        in_specs=[SMEM] + [VMEM] * 6,
        out_specs=(VMEM,) * 3,
        scratch_shapes=[pltpu.VMEM((6, 64, 128), F32)] + scratch,
        compiler_params=params,
    )(place, got, right, near, spread, normed, output_gate)
    sent = pl.pallas_call(
        far_kernel,
        name="far",
        out_shape=message,
        in_specs=[SMEM] + [VMEM] * 5,
        out_specs=VMEM,
        scratch_shapes=[pltpu.VMEM((6, 64, 128), F32)],
        input_output_aliases={5: 0},
        compiler_params=params,
    )(place, left, far, both, spread, sent)
    got = lax.all_to_all(sent, BOTH, 0, 0, axis_index_groups=SHARING)
    return pl.pallas_call(
        update_kernel,
        name="update",
        out_shape=struct((rows, cols, width), BF16),
        in_specs=[VMEM] * 4,
        out_specs=VMEM,
        scratch_shapes=[pltpu.VMEM((3, 256, 128), F32), pltpu.VMEM((rows * cols, 128), F32)],
        compiler_params=params,
    )(got, gate, columns, output_weight)


def solution(mesh):
    placed = (P("ia", "ja", None),) + (P(),) * 11
    return jax.shard_map(shards, mesh=mesh, in_specs=placed, out_specs=P("ia", "ja", None), check_vma=False)
```

```python
import jax
import jax.numpy as jnp
from jax import lax
from jax.experimental import pallas as pl
from jax.experimental.pallas import tpu as pltpu
from jax.sharding import PartitionSpec as P

BOTH = ("ia", "ja")
EPS = 1e-5
WIDE = 32
F32 = jnp.float32
BF16 = jnp.bfloat16
VMEM = pl.BlockSpec(memory_space=pltpu.VMEM)
SMEM = pl.BlockSpec(memory_space=pltpu.SMEM)
HBM = pl.BlockSpec(memory_space=pltpu.HBM)


def device(xl, y, core, xh, z):
    return (((xl * 8 + y) * 2 + core) * 2 + xh) * 8 + z


def fold(half, m):
    return m if half == 0 else 7 - m


SHARING = [
    [device(xl, fold(half, m), core, xh, z) for xl in range(2) for m in range(4) for xh in range(2) for z in range(8)]
    for half in range(2)
    for core in range(2)
]
PLACES = [(xl, y, core, xh, z) for xl in range(2) for y in range(8) for core in range(2) for xh in range(2) for z in range(8)]
CORE_FLIP = [(device(xl, y, core, xh, z), device(xl, y, 1 - core, xh, z)) for xl, y, core, xh, z in PLACES]
HALF_FLIP = [(device(xl, y, core, xh, z), device(xl, 7 - y, core, xh, z)) for xl, y, core, xh, z in PLACES]


def sigmoid(x):
    return 1.0 / (1.0 + jnp.exp(-x))


def iota(shape, axis):
    return lax.broadcasted_iota(jnp.int32, shape, axis)


def contract(a, b, da, db):
    return lax.dot_general(a, b, (((da,), (db,)), ((), ())), preferred_element_type=F32)


def edges_kernel(
    place_ref,
    pair_hbm,
    mask_hbm,
    gain_hbm,
    bias_hbm,
    out_gain_hbm,
    out_bias_hbm,
    lg_hbm,
    lv_hbm,
    rg_hbm,
    rv_hbm,
    sent_ref,
    normed_ref,
    columns_ref,
    spread_ref,
    pair_ref,
    mask_ref,
    gain_ref,
    bias_ref,
    out_gain_ref,
    out_bias_ref,
    lg_ref,
    lv_ref,
    rg_ref,
    rv_ref,
    rows_ref,
    arrived,
):
    fetches = [
        (pair_hbm, pair_ref),
        (mask_hbm, mask_ref),
        (gain_hbm, gain_ref),
        (bias_hbm, bias_ref),
        (lg_hbm, lg_ref),
        (lv_hbm, lv_ref),
        (rg_hbm, rg_ref),
        (rv_hbm, rv_ref),
        (out_gain_hbm, out_gain_ref),
        (out_bias_hbm, out_bias_ref),
    ]
    copies = [pltpu.make_async_copy(source, to, arrived.at[n]) for n, (source, to) in enumerate(fetches)]
    for copy in copies:
        copy.start()
    row = iota(spread_ref.shape, 0)
    side = jnp.where(row >= 96, 1, 0)
    row = row - 96 * side
    run = sum(jnp.where(row >= 12 * n, 1, 0) for n in range(1, 8))
    core = place_ref[2]
    to_lane = row + 20 * run + 16 * jnp.where(side == 0, core, 1 - core)
    spread_ref[...] = jnp.where(iota(spread_ref.shape, 1) == to_lane, 1.0, 0.0).astype(BF16)
    for copy in copies[:4]:
        copy.wait()
    width = lg_ref.shape[0]
    rows, cols = 12, 24
    x = pair_ref[...].astype(F32)
    mean = jnp.mean(x, axis=-1, keepdims=True)
    centered = x - mean
    variance = jnp.mean(centered * centered, axis=-1, keepdims=True)
    normed = centered * lax.rsqrt(variance + EPS) * gain_ref[...] + bias_ref[...]
    normed_ref[...] = normed.astype(BF16)
    place = iota((cols, width), 0)
    col_valid = jnp.zeros((cols, width), F32)
    for k in range(cols):
        col_valid = jnp.where(place == k, mask_ref[place_ref[1] + k].astype(F32), col_valid)
    parts = []
    for i in [3 * ii + iq for iq in range(3) for ii in range(4)]:
        row_valid = mask_ref[place_ref[0] + i].astype(F32)
        parts.append(normed[i * cols : (i + 1) * cols] * (col_valid * row_valid))
        parts.append(jnp.zeros((WIDE - cols, width), F32))
    masked = jnp.concatenate(parts, axis=0).astype(BF16)
    for copy in copies[4:]:
        copy.wait()
    left = sigmoid(contract(lg_ref[...], masked, 0, 1)) * contract(lv_ref[...], masked, 0, 1)
    right = sigmoid(contract(rg_ref[...], masked, 0, 1)) * contract(rv_ref[...], masked, 0, 1)
    for t in range(3):
        lanes = slice(t * 128, (t + 1) * 128)
        rows_ref[t, pl.ds(0, width, stride=2), :] = right[:, lanes]
        rows_ref[t, pl.ds(1, width, stride=2), :] = left[:, lanes]
        sent_ref[:, :, lanes] = rows_ref[t].astype(BF16).reshape(width, 2, 128)
    columns_ref[0] = jnp.transpose(jnp.broadcast_to(out_gain_ref[...], (width, width)))
    columns_ref[1] = jnp.transpose(jnp.broadcast_to(out_bias_ref[...], (width, width)))


def swap_blocks(blocks, lane):
    out = []
    for b in range(4):
        total = None
        for a in range(4):
            moved = blocks[a] if a == b else pltpu.roll(blocks[a], (WIDE * (a - b)) % 128, blocks[a].ndim - 1)
            total = moved if total is None else jnp.where(lane // WIDE == a, moved, total)
        out.append(total)
    return out


def spread_side(side, got_ref, rows_ref, quads_ref):
    lane = iota((32, 128), 1)
    wide = iota((8, 128), 1) % WIDE < 24
    spread = {}
    for iq in range(3):
        rows_ref[iq] = got_ref[:, :, iq * 128 : (iq + 1) * 128].astype(F32).reshape(256, 128)
        blocks = [rows_ref[iq, pl.ds(2 * k + side, 32, stride=8), :] for k in range(4)]
        for ii, block in enumerate(swap_blocks(blocks, lane)):
            at = (iq * 4 + ii) * 32
            quads_ref[pl.ds(at, 32), :] = block
            found = [quads_ref[pl.ds(at + quad, 8, stride=4), :] for quad in range(4)]
            spread[iq, ii] = [jnp.where(wide, found[v], pltpu.roll(found[3], 24 - 8 * v, 1)) for v in range(3)]
    return spread


def right_kernel(got_ref, right_ref, rows_ref, quads_ref, dense_ref):
    for (iq, ii), dense in spread_side(0, got_ref, rows_ref, quads_ref).items():
        for v in range(3):
            dense_ref[v, pl.ds(ii * 3 + iq, 8, stride=12), :] = dense[v]
    for v in range(3):
        right_ref[:, v * 128 : (v + 1) * 128] = dense_ref[v].astype(BF16)


def mix_half(place_ref, other, left_ref, mine_ref, theirs_ref, spread_ref, rows_ref):
    lane = iota((8, 128), 1)
    half = place_ref[3 + other]
    mixed = contract(left_ref[...], jnp.concatenate([mine_ref[...], theirs_ref[...]], axis=0), 1, 1)
    high = mixed.astype(BF16)
    low = (mixed - high.astype(F32)).astype(BF16)
    parts = contract(jnp.concatenate([high, low], axis=0), spread_ref[...], 1, 0)
    for xl in range(2):
        for iq in range(3):
            for part in range(2):
                at = part * 96 + iq * 32
                blocks = [parts[at + ii * 8 : at + (ii + 1) * 8, xl * 128 : (xl + 1) * 128] for ii in range(4)]
                for m, block in enumerate(swap_blocks(blocks, lane)):
                    to = (xl * 8 + m + half * (7 - 2 * m)) * 2 + part
                    rows_ref[iq, pl.ds(to, 8, stride=32), :] = block


def near_kernel(
    place_ref,
    got_ref,
    mine_ref,
    theirs_ref,
    spread_ref,
    normed_ref,
    og_ref,
    rows_ref,
    gate_ref,
    left_ref,
    got_rows_ref,
    quads_ref,
):
    blocks = spread_side(1, got_ref, got_rows_ref, quads_ref)
    for iq in range(3):
        for v in range(3):
            block = jnp.concatenate([blocks[iq, ii][v] for ii in range(4)], axis=0)
            left_ref[iq * 32 : (iq + 1) * 32, v * 128 : (v + 1) * 128] = block.astype(BF16)
    gate_ref[...] = sigmoid(contract(normed_ref[...], og_ref[...], 1, 0))
    mix_half(place_ref, 0, left_ref, mine_ref, theirs_ref, spread_ref, rows_ref)


def far_kernel(place_ref, left_ref, mine_ref, theirs_ref, spread_ref, near_ref, rows_ref, sent_ref):
    del near_ref
    mix_half(place_ref, 1, left_ref, mine_ref, theirs_ref, spread_ref, rows_ref)
    for t in range(3):
        sent_ref[:, :, t * 128 : (t + 1) * 128] = rows_ref[t].astype(BF16).reshape(128, 2, 128)


def update_kernel(got_ref, gate_ref, columns_ref, weight_ref, out_ref, rows_ref, flat_ref):
    rows, cols, width = out_ref.shape
    gain = columns_ref[0][:, 0:1]
    bias = columns_ref[1][:, 0:1]
    for iq in range(3):
        rows_ref[iq] = got_ref[:, :, iq * 128 : (iq + 1) * 128].astype(F32).reshape(2 * width, 128)
        mixed = rows_ref[iq, pl.ds(0, width, stride=2), :] + rows_ref[iq, pl.ds(1, width, stride=2), :]
        mean = jnp.mean(mixed, axis=0, keepdims=True)
        centered = mixed - mean
        variance = jnp.mean(centered * centered, axis=0, keepdims=True)
        normed = (centered * lax.rsqrt(variance + EPS) * gain + bias).astype(BF16)
        output = contract(normed, weight_ref[...], 0, 0)
        for ii in range(4):
            at = (3 * ii + iq) * cols
            flat_ref[at : at + 12, :] = output[ii * WIDE : ii * WIDE + 12]
            flat_ref[at + 12 : at + 24, :] = output[ii * WIDE + 16 : ii * WIDE + 28]
    out_ref[...] = (gate_ref[...] * flat_ref[...]).astype(BF16).reshape(rows, cols, width)


def shards(
    pair,
    token_mask,
    norm_in_gain,
    norm_in_bias,
    left_gate,
    left_value,
    right_gate,
    right_value,
    output_gate,
    norm_out_gain,
    norm_out_bias,
    output_weight,
):
    rows, cols, width = pair.shape
    params = pltpu.CompilerParams(vmem_limit_bytes=32 * 1024 * 1024)
    row_block = lax.axis_index("ia")
    half = row_block // 8 % 2
    place = jnp.stack([row_block * rows, lax.axis_index("ja") * cols, row_block % 2, half, 1 - half]).astype(jnp.int32)
    struct = jax.ShapeDtypeStruct
    message = struct((width, 2, rows * WIDE), BF16)
    arrays = [pair.reshape(rows * cols, width), token_mask]
    arrays += [v.reshape(1, -1) for v in (norm_in_gain, norm_in_bias, norm_out_gain, norm_out_bias)]
    arrays += [left_gate, left_value, right_gate, right_value]
    fetched = [pltpu.VMEM(array.shape, array.dtype) for array in arrays]
    fetched[1] = pltpu.SMEM(token_mask.shape, token_mask.dtype)
    sent, normed, columns, spread = pl.pallas_call(
        edges_kernel,
        name="edges",
        out_shape=(
            message,
            struct((rows * cols, width), BF16),
            struct((2, width, width), F32),
            struct((192, 256), BF16),
        ),
        in_specs=[SMEM] + [HBM] * 10,
        out_specs=(VMEM,) * 4,
        scratch_shapes=fetched + [pltpu.VMEM((3, 256, 128), F32), pltpu.SemaphoreType.DMA((10,))],
        compiler_params=params,
    )(place, *[pltpu.with_memory_space_constraint(array, pltpu.HBM) for array in arrays])
    got = lax.all_to_all(sent, BOTH, 0, 0, axis_index_groups=SHARING)
    scratch = [pltpu.VMEM((3, 256, 128), F32), pltpu.VMEM((384, 128), F32)]
    right = pl.pallas_call(
        right_kernel,
        name="right",
        out_shape=struct((96, 384), BF16),
        in_specs=[VMEM],
        out_specs=VMEM,
        scratch_shapes=scratch + [pltpu.VMEM((3, 96, 128), F32)],
        compiler_params=params,
    )(got)
    near = lax.ppermute(right, BOTH, CORE_FLIP)
    far = lax.ppermute(right, BOTH, HALF_FLIP)
    both = lax.ppermute(far, BOTH, CORE_FLIP)
    near_rows, gate, left = pl.pallas_call(
        near_kernel,
        name="near",
        out_shape=(struct((3, 256, 128), F32), struct((rows * cols, width), F32), struct((96, 384), BF16)),
        in_specs=[SMEM] + [VMEM] * 6,
        out_specs=(VMEM,) * 3,
        scratch_shapes=scratch,
        compiler_params=params,
    )(place, got, right, near, spread, normed, output_gate)
    _, sent = pl.pallas_call(
        far_kernel,
        name="far",
        out_shape=(struct((3, 256, 128), F32), message),
        in_specs=[SMEM] + [VMEM] * 5,
        out_specs=(VMEM, VMEM),
        input_output_aliases={5: 0},
        compiler_params=params,
    )(place, left, far, both, spread, near_rows)
    got = lax.all_to_all(sent, BOTH, 0, 0, axis_index_groups=SHARING)
    return pl.pallas_call(
        update_kernel,
        name="update",
        out_shape=struct((rows, cols, width), BF16),
        in_specs=[VMEM] * 4,
        out_specs=VMEM,
        scratch_shapes=[pltpu.VMEM((3, 256, 128), F32), pltpu.VMEM((rows * cols, 128), F32)],
        compiler_params=params,
    )(got, gate, columns, output_weight)


def solution(mesh):
    placed = (P("ia", "ja", None),) + (P(),) * 11
    return jax.shard_map(shards, mesh=mesh, in_specs=placed, out_specs=P("ia", "ja", None), check_vma=False)
```

```python
import jax
import jax.numpy as jnp
from jax import lax
from jax.experimental import pallas as pl
from jax.experimental.pallas import tpu as pltpu
from jax.sharding import PartitionSpec as P

BOTH = ("ia", "ja")
EPS = 1e-5
WIDE = 32
F32 = jnp.float32
BF16 = jnp.bfloat16
VMEM = pl.BlockSpec(memory_space=pltpu.VMEM)
HBM = pl.BlockSpec(memory_space=pltpu.HBM)


def device(xl, y, core, xh, z):
    return (((xl * 8 + y) * 2 + core) * 2 + xh) * 8 + z


def fold(half, m):
    return m if half == 0 else 7 - m


SHARING = [
    [device(xl, fold(half, m), core, xh, z) for xl in range(2) for m in range(4) for xh in range(2) for z in range(8)]
    for half in range(2)
    for core in range(2)
]
PLACES = [(xl, y, core, xh, z) for xl in range(2) for y in range(8) for core in range(2) for xh in range(2) for z in range(8)]
CORE_FLIP = [(device(xl, y, core, xh, z), device(xl, y, 1 - core, xh, z)) for xl, y, core, xh, z in PLACES]
HALF_FLIP = [(device(xl, y, core, xh, z), device(xl, 7 - y, core, xh, z)) for xl, y, core, xh, z in PLACES]


def place_of():
    block = lax.axis_index("ia")
    return block * 12, lax.axis_index("ja") * 24, lax.rem(block, 2), lax.rem(lax.div(block, 8), 2)


def sigmoid(x):
    return 1.0 / (1.0 + jnp.exp(-x))


def iota(shape, axis):
    return lax.broadcasted_iota(jnp.int32, shape, axis)


def contract(a, b, da, db):
    return lax.dot_general(a, b, (((da,), (db,)), ((), ())), preferred_element_type=F32)


def edges_kernel(
    pair_hbm,
    mask_hbm,
    gain_hbm,
    bias_hbm,
    out_gain_hbm,
    out_bias_hbm,
    lg_hbm,
    lv_hbm,
    rg_hbm,
    rv_hbm,
    sent_ref,
    normed_ref,
    columns_ref,
    spread_ref,
    pair_ref,
    mask_ref,
    gain_ref,
    bias_ref,
    out_gain_ref,
    out_bias_ref,
    lg_ref,
    lv_ref,
    rg_ref,
    rv_ref,
    rows_ref,
    arrived,
):
    fetches = [
        (pair_hbm, pair_ref),
        (mask_hbm, mask_ref),
        (gain_hbm, gain_ref),
        (bias_hbm, bias_ref),
        (lg_hbm, lg_ref),
        (lv_hbm, lv_ref),
        (rg_hbm, rg_ref),
        (rv_hbm, rv_ref),
        (out_gain_hbm, out_gain_ref),
        (out_bias_hbm, out_bias_ref),
    ]
    copies = [pltpu.make_async_copy(source, to, arrived.at[n]) for n, (source, to) in enumerate(fetches)]
    for copy in copies:
        copy.start()
    row = iota(spread_ref.shape, 0)
    side = jnp.where(row >= 96, 1, 0)
    row = row - 96 * side
    run = sum(jnp.where(row >= 12 * n, 1, 0) for n in range(1, 8))
    first_row, first_col, core, _ = place_of()
    to_lane = row + 20 * run + 16 * jnp.where(side == 0, core, 1 - core)
    spread_ref[...] = jnp.where(iota(spread_ref.shape, 1) == to_lane, 1.0, 0.0).astype(BF16)
    for copy in copies[:4]:
        copy.wait()
    width = lg_ref.shape[0]
    rows, cols = 12, 24
    x = pair_ref[...].astype(F32)
    mean = jnp.mean(x, axis=-1, keepdims=True)
    centered = x - mean
    variance = jnp.mean(centered * centered, axis=-1, keepdims=True)
    normed = centered * lax.rsqrt(variance + EPS) * gain_ref[...] + bias_ref[...]
    normed_ref[...] = normed.astype(BF16)
    place = iota((cols, width), 0)
    col_valid = jnp.zeros((cols, width), F32)
    for k in range(cols):
        col_valid = jnp.where(place == k, mask_ref[first_col + k].astype(F32), col_valid)
    parts = []
    for i in [3 * ii + iq for iq in range(3) for ii in range(4)]:
        row_valid = mask_ref[first_row + i].astype(F32)
        parts.append(normed[i * cols : (i + 1) * cols] * (col_valid * row_valid))
        parts.append(jnp.zeros((WIDE - cols, width), F32))
    masked = jnp.concatenate(parts, axis=0).astype(BF16)
    for copy in copies[4:]:
        copy.wait()
    left = sigmoid(contract(lg_ref[...], masked, 0, 1)) * contract(lv_ref[...], masked, 0, 1)
    right = sigmoid(contract(rg_ref[...], masked, 0, 1)) * contract(rv_ref[...], masked, 0, 1)
    for t in range(3):
        lanes = slice(t * 128, (t + 1) * 128)
        rows_ref[t, pl.ds(0, width, stride=2), :] = right[:, lanes]
        rows_ref[t, pl.ds(1, width, stride=2), :] = left[:, lanes]
        sent_ref[:, :, lanes] = rows_ref[t].astype(BF16).reshape(width, 2, 128)
    columns_ref[0] = jnp.transpose(jnp.broadcast_to(out_gain_ref[...], (width, width)))
    columns_ref[1] = jnp.transpose(jnp.broadcast_to(out_bias_ref[...], (width, width)))


def swap_blocks(blocks, lane):
    out = []
    for b in range(4):
        total = None
        for a in range(4):
            moved = blocks[a] if a == b else pltpu.roll(blocks[a], (WIDE * (a - b)) % 128, blocks[a].ndim - 1)
            total = moved if total is None else jnp.where(lane // WIDE == a, moved, total)
        out.append(total)
    return out


def spread_side(side, got_ref, rows_ref, quads_ref):
    lane = iota((32, 128), 1)
    wide = iota((8, 128), 1) % WIDE < 24
    spread = {}
    for iq in range(3):
        rows_ref[iq] = got_ref[:, :, iq * 128 : (iq + 1) * 128].astype(F32).reshape(256, 128)
        blocks = [rows_ref[iq, pl.ds(2 * k + side, 32, stride=8), :] for k in range(4)]
        for ii, block in enumerate(swap_blocks(blocks, lane)):
            at = (iq * 4 + ii) * 32
            quads_ref[pl.ds(at, 32), :] = block
            found = [quads_ref[pl.ds(at + quad, 8, stride=4), :] for quad in range(4)]
            spread[iq, ii] = [jnp.where(wide, found[v], pltpu.roll(found[3], 24 - 8 * v, 1)) for v in range(3)]
    return spread


def right_kernel(got_ref, right_ref, rows_ref, quads_ref, dense_ref):
    for (iq, ii), dense in spread_side(0, got_ref, rows_ref, quads_ref).items():
        for v in range(3):
            dense_ref[v, pl.ds(ii * 3 + iq, 8, stride=12), :] = dense[v]
    for v in range(3):
        right_ref[:, v * 128 : (v + 1) * 128] = dense_ref[v].astype(BF16)


def mix_half(other, left_ref, mine_ref, theirs_ref, spread_ref, sent_ref, slots_ref):
    lane = iota((8, 128), 1)
    half = place_of()[3]
    half = 1 - half if other else half
    mixed = contract(left_ref[...], jnp.concatenate([mine_ref[...], theirs_ref[...]], axis=0), 1, 1)
    high = mixed.astype(BF16)
    low = (mixed - high.astype(F32)).astype(BF16)
    parts = contract(jnp.concatenate([high, low], axis=0), spread_ref[...], 1, 0)
    for xl in range(2):
        for iq in range(3):
            for part in range(2):
                at = part * 96 + iq * 32
                blocks = [parts[at + ii * 8 : at + (ii + 1) * 8, xl * 128 : (xl + 1) * 128] for ii in range(4)]
                for m, block in enumerate(swap_blocks(blocks, lane)):
                    slot = (m + half * (3 - 2 * m)) * 2 + part
                    slots_ref[xl * 3 + iq, pl.ds(pl.multiple_of(slot * 8, 8), 8), :] = block
            for g in range(8):
                rows = slots_ref[xl * 3 + iq, pl.ds(g, 8, stride=8), :]
                to = g * 16 + xl * 8 + half * 4
                sent_ref[pl.ds(to, 4), :, iq * 128 : (iq + 1) * 128] = rows.astype(BF16).reshape(4, 2, 128)


def near_kernel(
    got_ref,
    mine_ref,
    theirs_ref,
    spread_ref,
    normed_ref,
    og_ref,
    sent_ref,
    gate_ref,
    left_ref,
    slots_ref,
    rows_ref,
    quads_ref,
):
    blocks = spread_side(1, got_ref, rows_ref, quads_ref)
    for iq in range(3):
        for v in range(3):
            block = jnp.concatenate([blocks[iq, ii][v] for ii in range(4)], axis=0)
            left_ref[iq * 32 : (iq + 1) * 32, v * 128 : (v + 1) * 128] = block.astype(BF16)
    gate_ref[...] = sigmoid(contract(normed_ref[...], og_ref[...], 1, 0))
    mix_half(0, left_ref, mine_ref, theirs_ref, spread_ref, sent_ref, slots_ref)


def far_kernel(left_ref, mine_ref, theirs_ref, spread_ref, half_ref, sent_ref, slots_ref):
    del half_ref
    mix_half(1, left_ref, mine_ref, theirs_ref, spread_ref, sent_ref, slots_ref)


def update_kernel(got_ref, gate_ref, columns_ref, weight_ref, out_ref, rows_ref, flat_ref):
    rows, cols, width = out_ref.shape
    gain = columns_ref[0][:, 0:1]
    bias = columns_ref[1][:, 0:1]
    for iq in range(3):
        rows_ref[iq] = got_ref[:, :, iq * 128 : (iq + 1) * 128].astype(F32).reshape(2 * width, 128)
        mixed = rows_ref[iq, pl.ds(0, width, stride=2), :] + rows_ref[iq, pl.ds(1, width, stride=2), :]
        mean = jnp.mean(mixed, axis=0, keepdims=True)
        centered = mixed - mean
        variance = jnp.mean(centered * centered, axis=0, keepdims=True)
        normed = (centered * lax.rsqrt(variance + EPS) * gain + bias).astype(BF16)
        output = contract(normed, weight_ref[...], 0, 0)
        for ii in range(4):
            at = (3 * ii + iq) * cols
            flat_ref[at : at + 12, :] = output[ii * WIDE : ii * WIDE + 12]
            flat_ref[at + 12 : at + 24, :] = output[ii * WIDE + 16 : ii * WIDE + 28]
    out_ref[...] = (gate_ref[...] * flat_ref[...]).astype(BF16).reshape(rows, cols, width)


def shards(
    pair,
    token_mask,
    norm_in_gain,
    norm_in_bias,
    left_gate,
    left_value,
    right_gate,
    right_value,
    output_gate,
    norm_out_gain,
    norm_out_bias,
    output_weight,
):
    rows, cols, width = pair.shape
    params = pltpu.CompilerParams(vmem_limit_bytes=32 * 1024 * 1024)
    struct = jax.ShapeDtypeStruct
    message = struct((width, 2, rows * WIDE), BF16)
    arrays = [pair.reshape(rows * cols, width), token_mask]
    arrays += [v.reshape(1, -1) for v in (norm_in_gain, norm_in_bias, norm_out_gain, norm_out_bias)]
    arrays += [left_gate, left_value, right_gate, right_value]
    fetched = [pltpu.VMEM(array.shape, array.dtype) for array in arrays]
    fetched[1] = pltpu.SMEM(token_mask.shape, token_mask.dtype)
    sent, normed, columns, spread = pl.pallas_call(
        edges_kernel,
        name="edges",
        out_shape=(
            message,
            struct((rows * cols, width), BF16),
            struct((2, width, width), F32),
            struct((192, 256), BF16),
        ),
        in_specs=[HBM] * 10,
        out_specs=(VMEM,) * 4,
        scratch_shapes=fetched + [pltpu.VMEM((3, 256, 128), F32), pltpu.SemaphoreType.DMA((10,))],
        compiler_params=params,
    )(*[pltpu.with_memory_space_constraint(array, pltpu.HBM) for array in arrays])
    got = lax.all_to_all(sent, BOTH, 0, 0, axis_index_groups=SHARING)
    scratch = [pltpu.VMEM((3, 256, 128), F32), pltpu.VMEM((384, 128), F32)]
    right = pl.pallas_call(
        right_kernel,
        name="right",
        out_shape=struct((96, 384), BF16),
        in_specs=[VMEM],
        out_specs=VMEM,
        scratch_shapes=scratch + [pltpu.VMEM((3, 96, 128), F32)],
        compiler_params=params,
    )(got)
    near = lax.ppermute(right, BOTH, CORE_FLIP)
    far = lax.ppermute(right, BOTH, HALF_FLIP)
    both = lax.ppermute(far, BOTH, CORE_FLIP)
    sent, gate, left = pl.pallas_call(
        near_kernel,
        name="near",
        out_shape=(message, struct((rows * cols, width), F32), struct((96, 384), BF16)),
        in_specs=[VMEM] * 6,
        out_specs=(VMEM,) * 3,
        scratch_shapes=[pltpu.VMEM((6, 64, 128), F32)] + scratch,
        compiler_params=params,
    )(got, right, near, spread, normed, output_gate)
    sent = pl.pallas_call(
        far_kernel,
        name="far",
        out_shape=message,
        in_specs=[VMEM] * 5,
        out_specs=VMEM,
        scratch_shapes=[pltpu.VMEM((6, 64, 128), F32)],
        input_output_aliases={4: 0},
        compiler_params=params,
    )(left, far, both, spread, sent)
    got = lax.all_to_all(sent, BOTH, 0, 0, axis_index_groups=SHARING)
    return pl.pallas_call(
        update_kernel,
        name="update",
        out_shape=struct((rows, cols, width), BF16),
        in_specs=[VMEM] * 4,
        out_specs=VMEM,
        scratch_shapes=[pltpu.VMEM((3, 256, 128), F32), pltpu.VMEM((rows * cols, 128), F32)],
        compiler_params=params,
    )(got, gate, columns, output_weight)


def solution(mesh):
    placed = (P("ia", "ja", None),) + (P(),) * 11
    return jax.shard_map(shards, mesh=mesh, in_specs=placed, out_specs=P("ia", "ja", None), check_vma=False)
```

```python
import jax
import jax.numpy as jnp
from jax import lax
from jax.experimental import pallas as pl
from jax.experimental.pallas import tpu as pltpu
from jax.sharding import PartitionSpec as P

BOTH = ("ia", "ja")
EPS = 1e-5
WIDE = 32
F32 = jnp.float32
BF16 = jnp.bfloat16
VMEM = pl.BlockSpec(memory_space=pltpu.VMEM)
HBM = pl.BlockSpec(memory_space=pltpu.HBM)


def device(xl, y, core, xh, z):
    return (((xl * 8 + y) * 2 + core) * 2 + xh) * 8 + z


def fold(half, m):
    return m if half == 0 else 7 - m


SHARING = [
    [device(xl, fold(half, m), core, xh, z) for xl in range(2) for m in range(4) for xh in range(2) for z in range(8)]
    for half in range(2)
    for core in range(2)
]
PLACES = [(xl, y, core, xh, z) for xl in range(2) for y in range(8) for core in range(2) for xh in range(2) for z in range(8)]
CORE_FLIP = [(device(xl, y, core, xh, z), device(xl, y, 1 - core, xh, z)) for xl, y, core, xh, z in PLACES]
HALF_FLIP = [(device(xl, y, core, xh, z), device(xl, 7 - y, core, xh, z)) for xl, y, core, xh, z in PLACES]


def place_of():
    block = lax.axis_index("ia")
    return block * 12, lax.axis_index("ja") * 24, lax.rem(block, 2), lax.rem(lax.div(block, 8), 2)


def sigmoid(x):
    return 1.0 / (1.0 + jnp.exp(-x))


def iota(shape, axis):
    return lax.broadcasted_iota(jnp.int32, shape, axis)


def contract(a, b, da, db):
    return lax.dot_general(a, b, (((da,), (db,)), ((), ())), preferred_element_type=F32)


def edges_kernel(
    pair_hbm,
    mask_hbm,
    gain_hbm,
    bias_hbm,
    out_gain_hbm,
    out_bias_hbm,
    lg_hbm,
    lv_hbm,
    rg_hbm,
    rv_hbm,
    sent_ref,
    normed_ref,
    columns_ref,
    spread_ref,
    pair_ref,
    mask_ref,
    gain_ref,
    bias_ref,
    out_gain_ref,
    out_bias_ref,
    lg_ref,
    lv_ref,
    rg_ref,
    rv_ref,
    rows_ref,
    arrived,
):
    fetches = [
        (pair_hbm, pair_ref),
        (mask_hbm, mask_ref),
        (gain_hbm, gain_ref),
        (bias_hbm, bias_ref),
        (lg_hbm, lg_ref),
        (lv_hbm, lv_ref),
        (rg_hbm, rg_ref),
        (rv_hbm, rv_ref),
        (out_gain_hbm, out_gain_ref),
        (out_bias_hbm, out_bias_ref),
    ]
    copies = [pltpu.make_async_copy(source, to, arrived.at[n]) for n, (source, to) in enumerate(fetches)]
    for copy in copies:
        copy.start()
    row = iota(spread_ref.shape, 0)
    side = jnp.where(row >= 96, 1, 0)
    row = row - 96 * side
    run = sum(jnp.where(row >= 12 * n, 1, 0) for n in range(1, 8))
    first_row, first_col, core, _ = place_of()
    to_lane = row + 20 * run + 16 * jnp.where(side == 0, core, 1 - core)
    spread_ref[...] = jnp.where(iota(spread_ref.shape, 1) == to_lane, 1.0, 0.0).astype(BF16)
    for copy in copies[:4]:
        copy.wait()
    width = lg_ref.shape[0]
    rows, cols = 12, 24
    x = pair_ref[...].astype(F32)
    mean = jnp.mean(x, axis=-1, keepdims=True)
    centered = x - mean
    variance = jnp.mean(centered * centered, axis=-1, keepdims=True)
    normed = centered * lax.rsqrt(variance + EPS) * gain_ref[...] + bias_ref[...]
    normed_ref[...] = normed.astype(BF16)
    place = iota((cols, width), 0)
    col_valid = jnp.zeros((cols, width), F32)
    for k in range(cols):
        col_valid = jnp.where(place == k, mask_ref[first_col + k].astype(F32), col_valid)
    parts = []
    for i in [3 * ii + iq for iq in range(3) for ii in range(4)]:
        row_valid = mask_ref[first_row + i].astype(F32)
        parts.append(normed[i * cols : (i + 1) * cols] * (col_valid * row_valid))
        parts.append(jnp.zeros((WIDE - cols, width), F32))
    masked = jnp.concatenate(parts, axis=0).astype(BF16)
    for copy in copies[4:]:
        copy.wait()
    left = sigmoid(contract(lg_ref[...], masked, 0, 1)) * contract(lv_ref[...], masked, 0, 1)
    right = sigmoid(contract(rg_ref[...], masked, 0, 1)) * contract(rv_ref[...], masked, 0, 1)
    for t in range(3):
        lanes = slice(t * 128, (t + 1) * 128)
        rows_ref[t, pl.ds(0, width, stride=2), :] = right[:, lanes]
        rows_ref[t, pl.ds(1, width, stride=2), :] = left[:, lanes]
        sent_ref[:, :, lanes] = rows_ref[t].astype(BF16).reshape(width, 2, 128)
    columns_ref[0] = jnp.transpose(jnp.broadcast_to(out_gain_ref[...], (width, width)))
    columns_ref[1] = jnp.transpose(jnp.broadcast_to(out_bias_ref[...], (width, width)))


def swap_blocks(blocks, lane):
    axis = blocks[0].ndim - 1
    run = lane // WIDE
    for step in (2, 1):
        high = run // step % 2 == 1
        swapped = list(blocks)
        for a in range(4):
            b = a + step
            if a // step % 2 == 0:
                swapped[a] = jnp.where(high, pltpu.roll(blocks[b], step * WIDE, axis), blocks[a])
                swapped[b] = jnp.where(high, blocks[b], pltpu.roll(blocks[a], 128 - step * WIDE, axis))
        blocks = swapped
    return blocks


def spread_side(side, got_ref, rows_ref, quads_ref):
    lane = iota((32, 128), 1)
    wide = iota((8, 128), 1) % WIDE < 24
    spread = {}
    for iq in range(3):
        rows_ref[iq] = got_ref[:, :, iq * 128 : (iq + 1) * 128].astype(F32).reshape(256, 128)
        blocks = [rows_ref[iq, pl.ds(2 * k + side, 32, stride=8), :] for k in range(4)]
        for ii, block in enumerate(swap_blocks(blocks, lane)):
            at = (iq * 4 + ii) * 32
            quads_ref[pl.ds(at, 32), :] = block
            found = [quads_ref[pl.ds(at + quad, 8, stride=4), :] for quad in range(4)]
            spread[iq, ii] = [jnp.where(wide, found[v], pltpu.roll(found[3], 24 - 8 * v, 1)) for v in range(3)]
    return spread


def right_kernel(got_ref, right_ref, rows_ref, quads_ref, dense_ref):
    for (iq, ii), dense in spread_side(0, got_ref, rows_ref, quads_ref).items():
        for v in range(3):
            dense_ref[v, pl.ds(ii * 3 + iq, 8, stride=12), :] = dense[v]
    for v in range(3):
        right_ref[:, v * 128 : (v + 1) * 128] = dense_ref[v].astype(BF16)


def mix_block(left_ref, right_ref, spread):
    mixed = contract(left_ref[...], right_ref[...], 1, 1)
    high = mixed.astype(BF16)
    low = (mixed - high.astype(F32)).astype(BF16)
    return contract(jnp.concatenate([high, low], axis=0), spread, 1, 0)


def write_half(other, parts, sent_ref, slots_ref):
    lane = iota((8, 128), 1)
    half = place_of()[3]
    half = 1 - half if other else half
    for xl in range(2):
        for iq in range(3):
            for part in range(2):
                at = part * 96 + iq * 32
                blocks = [parts[at + ii * 8 : at + (ii + 1) * 8, xl * 128 : (xl + 1) * 128] for ii in range(4)]
                for m, block in enumerate(swap_blocks(blocks, lane)):
                    slot = (m + half * (3 - 2 * m)) * 2 + part
                    slots_ref[xl * 3 + iq, pl.ds(pl.multiple_of(slot * 8, 8), 8), :] = block
            for g in range(8):
                rows = slots_ref[xl * 3 + iq, pl.ds(g, 8, stride=8), :]
                to = g * 16 + xl * 8 + half * 4
                sent_ref[pl.ds(to, 4), :, iq * 128 : (iq + 1) * 128] = rows.astype(BF16).reshape(4, 2, 128)


def near_kernel(
    got_ref,
    mine_ref,
    theirs_ref,
    far_ref,
    spread_ref,
    normed_ref,
    og_ref,
    sent_ref,
    gate_ref,
    left_ref,
    parts_ref,
    slots_ref,
    rows_ref,
    quads_ref,
):
    blocks = spread_side(1, got_ref, rows_ref, quads_ref)
    for iq in range(3):
        for v in range(3):
            block = jnp.concatenate([blocks[iq, ii][v] for ii in range(4)], axis=0)
            left_ref[iq * 32 : (iq + 1) * 32, v * 128 : (v + 1) * 128] = block.astype(BF16)
    gate_ref[...] = sigmoid(contract(normed_ref[...], og_ref[...], 1, 0))
    mine, theirs = spread_ref[0:96], spread_ref[96:192]
    parts = mix_block(left_ref, mine_ref, mine) + mix_block(left_ref, theirs_ref, theirs)
    write_half(0, parts, sent_ref, slots_ref)
    parts_ref[...] = mix_block(left_ref, far_ref, mine)


def far_kernel(left_ref, theirs_ref, spread_ref, parts_ref, half_ref, sent_ref, slots_ref):
    del half_ref
    parts = parts_ref[...] + mix_block(left_ref, theirs_ref, spread_ref[96:192])
    write_half(1, parts, sent_ref, slots_ref)


def update_kernel(got_ref, gate_ref, columns_ref, weight_ref, out_ref, rows_ref, flat_ref):
    rows, cols, width = out_ref.shape
    gain = columns_ref[0][:, 0:1]
    bias = columns_ref[1][:, 0:1]
    for iq in range(3):
        rows_ref[iq] = got_ref[:, :, iq * 128 : (iq + 1) * 128].astype(F32).reshape(2 * width, 128)
        mixed = rows_ref[iq, pl.ds(0, width, stride=2), :] + rows_ref[iq, pl.ds(1, width, stride=2), :]
        mean = jnp.mean(mixed, axis=0, keepdims=True)
        centered = mixed - mean
        variance = jnp.mean(centered * centered, axis=0, keepdims=True)
        normed = (centered * lax.rsqrt(variance + EPS) * gain + bias).astype(BF16)
        output = contract(normed, weight_ref[...], 0, 0)
        for ii in range(4):
            at = (3 * ii + iq) * cols
            flat_ref[at : at + 12, :] = output[ii * WIDE : ii * WIDE + 12]
            flat_ref[at + 12 : at + 24, :] = output[ii * WIDE + 16 : ii * WIDE + 28]
    out_ref[...] = (gate_ref[...] * flat_ref[...]).astype(BF16).reshape(rows, cols, width)


def shards(
    pair,
    token_mask,
    norm_in_gain,
    norm_in_bias,
    left_gate,
    left_value,
    right_gate,
    right_value,
    output_gate,
    norm_out_gain,
    norm_out_bias,
    output_weight,
):
    rows, cols, width = pair.shape
    params = pltpu.CompilerParams(vmem_limit_bytes=32 * 1024 * 1024)
    struct = jax.ShapeDtypeStruct
    message = struct((width, 2, rows * WIDE), BF16)
    arrays = [pair.reshape(rows * cols, width), token_mask]
    arrays += [v.reshape(1, -1) for v in (norm_in_gain, norm_in_bias, norm_out_gain, norm_out_bias)]
    arrays += [left_gate, left_value, right_gate, right_value]
    fetched = [pltpu.VMEM(array.shape, array.dtype) for array in arrays]
    fetched[1] = pltpu.SMEM(token_mask.shape, token_mask.dtype)
    sent, normed, columns, spread = pl.pallas_call(
        edges_kernel,
        name="edges",
        out_shape=(
            message,
            struct((rows * cols, width), BF16),
            struct((2, width, width), F32),
            struct((192, 256), BF16),
        ),
        in_specs=[HBM] * 10,
        out_specs=(VMEM,) * 4,
        scratch_shapes=fetched + [pltpu.VMEM((3, 256, 128), F32), pltpu.SemaphoreType.DMA((10,))],
        compiler_params=params,
    )(*[pltpu.with_memory_space_constraint(array, pltpu.HBM) for array in arrays])
    got = lax.all_to_all(sent, BOTH, 0, 0, axis_index_groups=SHARING)
    scratch = [pltpu.VMEM((3, 256, 128), F32), pltpu.VMEM((384, 128), F32)]
    right = pl.pallas_call(
        right_kernel,
        name="right",
        out_shape=struct((96, 384), BF16),
        in_specs=[VMEM],
        out_specs=VMEM,
        scratch_shapes=scratch + [pltpu.VMEM((3, 96, 128), F32)],
        compiler_params=params,
    )(got)
    near = lax.ppermute(right, BOTH, CORE_FLIP)
    far = lax.ppermute(right, BOTH, HALF_FLIP)
    both = lax.ppermute(far, BOTH, CORE_FLIP)
    sent, gate, left, parts = pl.pallas_call(
        near_kernel,
        name="near",
        out_shape=(
            message,
            struct((rows * cols, width), F32),
            struct((96, 384), BF16),
            struct((192, 256), F32),
        ),
        in_specs=[VMEM] * 7,
        out_specs=(VMEM,) * 4,
        scratch_shapes=[pltpu.VMEM((6, 64, 128), F32)] + scratch,
        compiler_params=params,
    )(got, right, near, far, spread, normed, output_gate)
    sent = pl.pallas_call(
        far_kernel,
        name="far",
        out_shape=message,
        in_specs=[VMEM] * 5,
        out_specs=VMEM,
        scratch_shapes=[pltpu.VMEM((6, 64, 128), F32)],
        input_output_aliases={4: 0},
        compiler_params=params,
    )(left, both, spread, parts, sent)
    got = lax.all_to_all(sent, BOTH, 0, 0, axis_index_groups=SHARING)
    return pl.pallas_call(
        update_kernel,
        name="update",
        out_shape=struct((rows, cols, width), BF16),
        in_specs=[VMEM] * 4,
        out_specs=VMEM,
        scratch_shapes=[pltpu.VMEM((3, 256, 128), F32), pltpu.VMEM((rows * cols, 128), F32)],
        compiler_params=params,
    )(got, gate, columns, output_weight)


def solution(mesh):
    placed = (P("ia", "ja", None),) + (P(),) * 11
    return jax.shard_map(shards, mesh=mesh, in_specs=placed, out_specs=P("ia", "ja", None), check_vma=False)
```

```python
import jax
import jax.numpy as jnp
from jax import lax
from jax.experimental import pallas as pl
from jax.experimental.pallas import tpu as pltpu
from jax.sharding import PartitionSpec as P

BOTH = ("ia", "ja")
EPS = 1e-5
WIDE = 32
F32 = jnp.float32
BF16 = jnp.bfloat16
VMEM = pl.BlockSpec(memory_space=pltpu.VMEM)
HBM = pl.BlockSpec(memory_space=pltpu.HBM)


def device(xl, y, core, xh, z):
    return (((xl * 8 + y) * 2 + core) * 2 + xh) * 8 + z


def fold(half, m):
    return m if half == 0 else 7 - m


SHARING = [
    [device(xl, fold(half, m), core, xh, z) for xl in range(2) for m in range(4) for xh in range(2) for z in range(8)]
    for half in range(2)
    for core in range(2)
]
PLACES = [(xl, y, core, xh, z) for xl in range(2) for y in range(8) for core in range(2) for xh in range(2) for z in range(8)]
CORE_FLIP = [(device(xl, y, core, xh, z), device(xl, y, 1 - core, xh, z)) for xl, y, core, xh, z in PLACES]
HALF_FLIP = [(device(xl, y, core, xh, z), device(xl, 7 - y, core, xh, z)) for xl, y, core, xh, z in PLACES]


def place_of():
    block = lax.axis_index("ia")
    return block * 12, lax.axis_index("ja") * 24, lax.rem(block, 2), lax.rem(lax.div(block, 8), 2)


def sigmoid(x):
    return 1.0 / (1.0 + jnp.exp(-x))


def iota(shape, axis):
    return lax.broadcasted_iota(jnp.int32, shape, axis)


def contract(a, b, da, db):
    return lax.dot_general(a, b, (((da,), (db,)), ((), ())), preferred_element_type=F32)


def edges_kernel(
    pair_hbm,
    mask_hbm,
    gain_hbm,
    bias_hbm,
    out_gain_hbm,
    out_bias_hbm,
    lg_hbm,
    lv_hbm,
    rg_hbm,
    rv_hbm,
    sent_ref,
    normed_ref,
    columns_ref,
    spread_ref,
    pair_ref,
    mask_ref,
    gain_ref,
    bias_ref,
    out_gain_ref,
    out_bias_ref,
    weights_ref,
    rows_ref,
    arrived,
):
    fetches = [
        (pair_hbm, pair_ref),
        (mask_hbm, mask_ref),
        (gain_hbm, gain_ref),
        (bias_hbm, bias_ref),
        (lg_hbm, weights_ref.at[:, 0:128]),
        (lv_hbm, weights_ref.at[:, 128:256]),
        (rg_hbm, weights_ref.at[:, 256:384]),
        (rv_hbm, weights_ref.at[:, 384:512]),
        (out_gain_hbm, out_gain_ref),
        (out_bias_hbm, out_bias_ref),
    ]
    copies = [pltpu.make_async_copy(source, to, arrived.at[n]) for n, (source, to) in enumerate(fetches)]
    for copy in copies:
        copy.start()
    row = iota(spread_ref.shape, 0)
    side = jnp.where(row >= 96, 1, 0)
    row = row - 96 * side
    run = sum(jnp.where(row >= 12 * n, 1, 0) for n in range(1, 8))
    first_row, first_col, core, _ = place_of()
    to_lane = row + 20 * run + 16 * jnp.where(side == 0, core, 1 - core)
    spread_ref[...] = jnp.where(iota(spread_ref.shape, 1) == to_lane, 1.0, 0.0).astype(BF16)
    for copy in copies[:4]:
        copy.wait()
    width = pair_ref.shape[1]
    rows, cols = 12, 24
    x = pair_ref[...].astype(F32)
    mean = jnp.mean(x, axis=-1, keepdims=True)
    centered = x - mean
    variance = jnp.mean(centered * centered, axis=-1, keepdims=True)
    normed = centered * lax.rsqrt(variance + EPS) * gain_ref[...] + bias_ref[...]
    normed_ref[...] = normed.astype(BF16)
    place = iota((cols, width), 0)
    col_valid = jnp.zeros((cols, width), F32)
    for k in range(cols):
        col_valid = jnp.where(place == k, mask_ref[first_col + k].astype(F32), col_valid)
    parts = []
    for i in [3 * ii + iq for iq in range(3) for ii in range(4)]:
        row_valid = mask_ref[first_row + i].astype(F32)
        parts.append(normed[i * cols : (i + 1) * cols] * (col_valid * row_valid))
        parts.append(jnp.zeros((WIDE - cols, width), F32))
    masked = jnp.concatenate(parts, axis=0).astype(BF16)
    for copy in copies[4:]:
        copy.wait()
    projected = contract(weights_ref[...], masked, 0, 1)
    left = sigmoid(projected[0:128]) * projected[128:256]
    right = sigmoid(projected[256:384]) * projected[384:512]
    for t in range(3):
        lanes = slice(t * 128, (t + 1) * 128)
        rows_ref[t, pl.ds(0, width, stride=2), :] = right[:, lanes]
        rows_ref[t, pl.ds(1, width, stride=2), :] = left[:, lanes]
        sent_ref[:, :, lanes] = rows_ref[t].astype(BF16).reshape(width, 2, 128)
    columns_ref[0] = jnp.transpose(jnp.broadcast_to(out_gain_ref[...], (width, width)))
    columns_ref[1] = jnp.transpose(jnp.broadcast_to(out_bias_ref[...], (width, width)))


def swap_blocks(blocks, lane):
    axis = blocks[0].ndim - 1
    run = lane // WIDE
    for step in (2, 1):
        high = run // step % 2 == 1
        swapped = list(blocks)
        for a in range(4):
            b = a + step
            if a // step % 2 == 0:
                swapped[a] = jnp.where(high, pltpu.roll(blocks[b], step * WIDE, axis), blocks[a])
                swapped[b] = jnp.where(high, blocks[b], pltpu.roll(blocks[a], 128 - step * WIDE, axis))
        blocks = swapped
    return blocks


def spread_side(side, got_ref, rows_ref, quads_ref):
    lane = iota((32, 128), 1)
    wide = iota((8, 128), 1) % WIDE < 24
    spread = {}
    for iq in range(3):
        rows_ref[iq] = got_ref[:, :, iq * 128 : (iq + 1) * 128].astype(F32).reshape(256, 128)
        blocks = [rows_ref[iq, pl.ds(2 * k + side, 32, stride=8), :] for k in range(4)]
        for ii, block in enumerate(swap_blocks(blocks, lane)):
            at = (iq * 4 + ii) * 32
            quads_ref[pl.ds(at, 32), :] = block
            found = [quads_ref[pl.ds(at + quad, 8, stride=4), :] for quad in range(4)]
            spread[iq, ii] = [jnp.where(wide, found[v], pltpu.roll(found[3], 24 - 8 * v, 1)) for v in range(3)]
    return spread


def right_kernel(got_ref, right_ref, rows_ref, quads_ref, dense_ref):
    for (iq, ii), dense in spread_side(0, got_ref, rows_ref, quads_ref).items():
        for v in range(3):
            dense_ref[v, pl.ds(ii * 3 + iq, 8, stride=12), :] = dense[v]
    for v in range(3):
        right_ref[:, v * 128 : (v + 1) * 128] = dense_ref[v].astype(BF16)


def mix_block(left_ref, right_ref, spread):
    mixed = contract(left_ref[...], right_ref[...], 1, 1)
    high = mixed.astype(BF16)
    low = (mixed - high.astype(F32)).astype(BF16)
    return contract(jnp.concatenate([high, low], axis=0), spread, 1, 0)


def write_half(other, parts, sent_ref, slots_ref):
    lane = iota((8, 128), 1)
    half = place_of()[3]
    half = 1 - half if other else half
    for xl in range(2):
        for iq in range(3):
            for part in range(2):
                at = part * 96 + iq * 32
                blocks = [parts[at + ii * 8 : at + (ii + 1) * 8, xl * 128 : (xl + 1) * 128] for ii in range(4)]
                for m, block in enumerate(swap_blocks(blocks, lane)):
                    slot = (m + half * (3 - 2 * m)) * 2 + part
                    slots_ref[xl * 3 + iq, pl.ds(pl.multiple_of(slot * 8, 8), 8), :] = block
            for g in range(8):
                rows = slots_ref[xl * 3 + iq, pl.ds(g, 8, stride=8), :]
                to = g * 16 + xl * 8 + half * 4
                sent_ref[pl.ds(to, 4), :, iq * 128 : (iq + 1) * 128] = rows.astype(BF16).reshape(4, 2, 128)


def near_kernel(
    got_ref,
    mine_ref,
    theirs_ref,
    far_ref,
    spread_ref,
    normed_ref,
    og_ref,
    sent_ref,
    gate_ref,
    left_ref,
    parts_ref,
    slots_ref,
    rows_ref,
    quads_ref,
):
    blocks = spread_side(1, got_ref, rows_ref, quads_ref)
    for iq in range(3):
        for v in range(3):
            block = jnp.concatenate([blocks[iq, ii][v] for ii in range(4)], axis=0)
            left_ref[iq * 32 : (iq + 1) * 32, v * 128 : (v + 1) * 128] = block.astype(BF16)
    gate_ref[...] = sigmoid(contract(normed_ref[...], og_ref[...], 1, 0))
    mine, theirs = spread_ref[0:96], spread_ref[96:192]
    parts = mix_block(left_ref, mine_ref, mine) + mix_block(left_ref, theirs_ref, theirs)
    write_half(0, parts, sent_ref, slots_ref)
    parts_ref[...] = mix_block(left_ref, far_ref, mine)


def far_kernel(left_ref, theirs_ref, spread_ref, parts_ref, half_ref, sent_ref, slots_ref):
    del half_ref
    parts = parts_ref[...] + mix_block(left_ref, theirs_ref, spread_ref[96:192])
    write_half(1, parts, sent_ref, slots_ref)


def update_kernel(got_ref, gate_ref, columns_ref, weight_ref, out_ref, rows_ref, flat_ref):
    rows, cols, width = out_ref.shape
    gain = columns_ref[0][:, 0:1]
    bias = columns_ref[1][:, 0:1]
    for iq in range(3):
        rows_ref[iq] = got_ref[:, :, iq * 128 : (iq + 1) * 128].astype(F32).reshape(2 * width, 128)
        mixed = rows_ref[iq, pl.ds(0, width, stride=2), :] + rows_ref[iq, pl.ds(1, width, stride=2), :]
        mean = jnp.mean(mixed, axis=0, keepdims=True)
        centered = mixed - mean
        variance = jnp.mean(centered * centered, axis=0, keepdims=True)
        normed = (centered * lax.rsqrt(variance + EPS) * gain + bias).astype(BF16)
        output = contract(normed, weight_ref[...], 0, 0)
        for ii in range(4):
            at = (3 * ii + iq) * cols
            flat_ref[at : at + 12, :] = output[ii * WIDE : ii * WIDE + 12]
            flat_ref[at + 12 : at + 24, :] = output[ii * WIDE + 16 : ii * WIDE + 28]
    out_ref[...] = (gate_ref[...] * flat_ref[...]).astype(BF16).reshape(rows, cols, width)


def shards(
    pair,
    token_mask,
    norm_in_gain,
    norm_in_bias,
    left_gate,
    left_value,
    right_gate,
    right_value,
    output_gate,
    norm_out_gain,
    norm_out_bias,
    output_weight,
):
    rows, cols, width = pair.shape
    params = pltpu.CompilerParams(vmem_limit_bytes=32 * 1024 * 1024)
    struct = jax.ShapeDtypeStruct
    message = struct((width, 2, rows * WIDE), BF16)
    arrays = [pair.reshape(rows * cols, width), token_mask]
    arrays += [v.reshape(1, -1) for v in (norm_in_gain, norm_in_bias, norm_out_gain, norm_out_bias)]
    arrays += [left_gate, left_value, right_gate, right_value]
    fetched = [pltpu.VMEM(array.shape, array.dtype) for array in arrays[:6]] + [pltpu.VMEM((width, 4 * width), BF16)]
    fetched[1] = pltpu.SMEM(token_mask.shape, token_mask.dtype)
    sent, normed, columns, spread = pl.pallas_call(
        edges_kernel,
        name="edges",
        out_shape=(
            message,
            struct((rows * cols, width), BF16),
            struct((2, width, width), F32),
            struct((192, 256), BF16),
        ),
        in_specs=[HBM] * 10,
        out_specs=(VMEM,) * 4,
        scratch_shapes=fetched + [pltpu.VMEM((3, 256, 128), F32), pltpu.SemaphoreType.DMA((10,))],
        compiler_params=params,
    )(*[pltpu.with_memory_space_constraint(array, pltpu.HBM) for array in arrays])
    got = lax.all_to_all(sent, BOTH, 0, 0, axis_index_groups=SHARING)
    scratch = [pltpu.VMEM((3, 256, 128), F32), pltpu.VMEM((384, 128), F32)]
    right = pl.pallas_call(
        right_kernel,
        name="right",
        out_shape=struct((96, 384), BF16),
        in_specs=[VMEM],
        out_specs=VMEM,
        scratch_shapes=scratch + [pltpu.VMEM((3, 96, 128), F32)],
        compiler_params=params,
    )(got)
    near = lax.ppermute(right, BOTH, CORE_FLIP)
    far = lax.ppermute(right, BOTH, HALF_FLIP)
    both = lax.ppermute(far, BOTH, CORE_FLIP)
    sent, gate, left, parts = pl.pallas_call(
        near_kernel,
        name="near",
        out_shape=(
            message,
            struct((rows * cols, width), F32),
            struct((96, 384), BF16),
            struct((192, 256), F32),
        ),
        in_specs=[VMEM] * 7,
        out_specs=(VMEM,) * 4,
        scratch_shapes=[pltpu.VMEM((6, 64, 128), F32)] + scratch,
        compiler_params=params,
    )(got, right, near, far, spread, normed, output_gate)
    sent = pl.pallas_call(
        far_kernel,
        name="far",
        out_shape=message,
        in_specs=[VMEM] * 5,
        out_specs=VMEM,
        scratch_shapes=[pltpu.VMEM((6, 64, 128), F32)],
        input_output_aliases={4: 0},
        compiler_params=params,
    )(left, both, spread, parts, sent)
    got = lax.all_to_all(sent, BOTH, 0, 0, axis_index_groups=SHARING)
    return pl.pallas_call(
        update_kernel,
        name="update",
        out_shape=struct((rows, cols, width), BF16),
        in_specs=[VMEM] * 4,
        out_specs=VMEM,
        scratch_shapes=[pltpu.VMEM((3, 256, 128), F32), pltpu.VMEM((rows * cols, 128), F32)],
        compiler_params=params,
    )(got, gate, columns, output_weight)


def solution(mesh):
    placed = (P("ia", "ja", None),) + (P(),) * 11
    return jax.shard_map(shards, mesh=mesh, in_specs=placed, out_specs=P("ia", "ja", None), check_vma=False)
```

```python
import jax
import jax.numpy as jnp
from jax import lax
from jax.experimental import pallas as pl
from jax.experimental.pallas import tpu as pltpu
from jax.sharding import PartitionSpec as P

BOTH = ("ia", "ja")
EPS = 1e-5
WIDE = 32
F32 = jnp.float32
BF16 = jnp.bfloat16
VMEM = pl.BlockSpec(memory_space=pltpu.VMEM)
HBM = pl.BlockSpec(memory_space=pltpu.HBM)


def device(xl, y, core, xh, z):
    return (((xl * 8 + y) * 2 + core) * 2 + xh) * 8 + z


def fold(half, m):
    return m if half == 0 else 7 - m


SHARING = [
    [device(xl, fold(half, m), core, xh, z) for xl in range(2) for m in range(4) for xh in range(2) for z in range(8)]
    for half in range(2)
    for core in range(2)
]
PLACES = [(xl, y, core, xh, z) for xl in range(2) for y in range(8) for core in range(2) for xh in range(2) for z in range(8)]
CORE_FLIP = [(device(xl, y, core, xh, z), device(xl, y, 1 - core, xh, z)) for xl, y, core, xh, z in PLACES]
HALF_FLIP = [(device(xl, y, core, xh, z), device(xl, 7 - y, core, xh, z)) for xl, y, core, xh, z in PLACES]


def place_of():
    block = lax.axis_index("ia")
    return block * 12, lax.axis_index("ja") * 24, lax.rem(block, 2), lax.rem(lax.div(block, 8), 2)


def sigmoid(x):
    return 1.0 / (1.0 + jnp.exp(-x))


def iota(shape, axis):
    return lax.broadcasted_iota(jnp.int32, shape, axis)


def contract(a, b, da, db):
    return lax.dot_general(a, b, (((da,), (db,)), ((), ())), preferred_element_type=F32)


def edges_kernel(
    pair_hbm,
    mask_hbm,
    gain_hbm,
    bias_hbm,
    out_gain_hbm,
    out_bias_hbm,
    lg_hbm,
    lv_hbm,
    rg_hbm,
    rv_hbm,
    sent_ref,
    normed_ref,
    columns_ref,
    spread_ref,
    pair_ref,
    mask_ref,
    gain_ref,
    bias_ref,
    out_gain_ref,
    out_bias_ref,
    lg_ref,
    lv_ref,
    rg_ref,
    rv_ref,
    rows_ref,
    arrived,
):
    fetches = [
        (pair_hbm, pair_ref),
        (mask_hbm, mask_ref),
        (gain_hbm, gain_ref),
        (bias_hbm, bias_ref),
        (lg_hbm, lg_ref),
        (lv_hbm, lv_ref),
        (rg_hbm, rg_ref),
        (rv_hbm, rv_ref),
        (out_gain_hbm, out_gain_ref),
        (out_bias_hbm, out_bias_ref),
    ]
    copies = [pltpu.make_async_copy(source, to, arrived.at[n]) for n, (source, to) in enumerate(fetches)]
    for copy in copies:
        copy.start()
    row = iota(spread_ref.shape, 0)
    side = jnp.where(row >= 96, 1, 0)
    row = row - 96 * side
    run = sum(jnp.where(row >= 12 * n, 1, 0) for n in range(1, 8))
    first_row, first_col, core, _ = place_of()
    to_lane = row + 20 * run + 16 * jnp.where(side == 0, core, 1 - core)
    spread_ref[...] = jnp.where(iota(spread_ref.shape, 1) == to_lane, 1.0, 0.0).astype(BF16)
    width = lg_ref.shape[0]
    rows, cols = 12, 24
    copies[1].wait()
    place = iota((cols, width), 0)
    col_valid = jnp.zeros((cols, width), F32)
    for k in range(cols):
        col_valid = jnp.where(place == k, mask_ref[first_col + k].astype(F32), col_valid)
    for copy in (copies[0], copies[2], copies[3]):
        copy.wait()
    x = pair_ref[...].astype(F32)
    mean = jnp.mean(x, axis=-1, keepdims=True)
    centered = x - mean
    variance = jnp.mean(centered * centered, axis=-1, keepdims=True)
    normed = centered * lax.rsqrt(variance + EPS) * gain_ref[...] + bias_ref[...]
    normed_ref[...] = normed.astype(BF16)
    parts = []
    for i in [3 * ii + iq for iq in range(3) for ii in range(4)]:
        row_valid = mask_ref[first_row + i].astype(F32)
        parts.append(normed[i * cols : (i + 1) * cols] * (col_valid * row_valid))
        parts.append(jnp.zeros((WIDE - cols, width), F32))
    masked = jnp.concatenate(parts, axis=0).astype(BF16)
    for copy in copies[4:]:
        copy.wait()
    left = sigmoid(contract(lg_ref[...], masked, 0, 1)) * contract(lv_ref[...], masked, 0, 1)
    right = sigmoid(contract(rg_ref[...], masked, 0, 1)) * contract(rv_ref[...], masked, 0, 1)
    for t in range(3):
        lanes = slice(t * 128, (t + 1) * 128)
        rows_ref[t, pl.ds(0, width, stride=2), :] = right[:, lanes]
        rows_ref[t, pl.ds(1, width, stride=2), :] = left[:, lanes]
        sent_ref[:, :, lanes] = rows_ref[t].astype(BF16).reshape(width, 2, 128)
    columns_ref[0] = jnp.transpose(jnp.broadcast_to(out_gain_ref[...], (width, width)))
    columns_ref[1] = jnp.transpose(jnp.broadcast_to(out_bias_ref[...], (width, width)))


def swap_blocks(blocks, lane):
    out = []
    for b in range(4):
        total = None
        for a in range(4):
            moved = blocks[a] if a == b else pltpu.roll(blocks[a], (WIDE * (a - b)) % 128, blocks[a].ndim - 1)
            total = moved if total is None else jnp.where(lane // WIDE == a, moved, total)
        out.append(total)
    return out


def spread_side(side, got_ref, rows_ref, quads_ref):
    lane = iota((32, 128), 1)
    wide = iota((8, 128), 1) % WIDE < 24
    spread = {}
    for iq in range(3):
        rows_ref[iq] = got_ref[:, :, iq * 128 : (iq + 1) * 128].astype(F32).reshape(256, 128)
        blocks = [rows_ref[iq, pl.ds(2 * k + side, 32, stride=8), :] for k in range(4)]
        for ii, block in enumerate(swap_blocks(blocks, lane)):
            at = (iq * 4 + ii) * 32
            quads_ref[pl.ds(at, 32), :] = block
            found = [quads_ref[pl.ds(at + quad, 8, stride=4), :] for quad in range(4)]
            spread[iq, ii] = [jnp.where(wide, found[v], pltpu.roll(found[3], 24 - 8 * v, 1)) for v in range(3)]
    return spread


def right_kernel(got_ref, right_ref, rows_ref, quads_ref, dense_ref):
    for (iq, ii), dense in spread_side(0, got_ref, rows_ref, quads_ref).items():
        for v in range(3):
            dense_ref[v, pl.ds(ii * 3 + iq, 8, stride=12), :] = dense[v]
    for v in range(3):
        right_ref[:, v * 128 : (v + 1) * 128] = dense_ref[v].astype(BF16)


def mix_half(other, left_ref, mine_ref, theirs_ref, spread_ref, sent_ref, slots_ref):
    lane = iota((8, 128), 1)
    half = place_of()[3]
    half = 1 - half if other else half
    mixed = contract(left_ref[...], jnp.concatenate([mine_ref[...], theirs_ref[...]], axis=0), 1, 1)
    high = mixed.astype(BF16)
    low = (mixed - high.astype(F32)).astype(BF16)
    parts = contract(jnp.concatenate([high, low], axis=0), spread_ref[...], 1, 0)
    for xl in range(2):
        for iq in range(3):
            for part in range(2):
                at = part * 96 + iq * 32
                blocks = [parts[at + ii * 8 : at + (ii + 1) * 8, xl * 128 : (xl + 1) * 128] for ii in range(4)]
                for m, block in enumerate(swap_blocks(blocks, lane)):
                    slot = (m + half * (3 - 2 * m)) * 2 + part
                    slots_ref[xl * 3 + iq, pl.ds(pl.multiple_of(slot * 8, 8), 8), :] = block
            for g in range(8):
                rows = slots_ref[xl * 3 + iq, pl.ds(g, 8, stride=8), :]
                to = g * 16 + xl * 8 + half * 4
                sent_ref[pl.ds(to, 4), :, iq * 128 : (iq + 1) * 128] = rows.astype(BF16).reshape(4, 2, 128)


def near_kernel(
    got_ref,
    mine_ref,
    theirs_ref,
    spread_ref,
    normed_ref,
    og_ref,
    sent_ref,
    gate_ref,
    left_ref,
    slots_ref,
    rows_ref,
    quads_ref,
):
    blocks = spread_side(1, got_ref, rows_ref, quads_ref)
    for iq in range(3):
        for v in range(3):
            block = jnp.concatenate([blocks[iq, ii][v] for ii in range(4)], axis=0)
            left_ref[iq * 32 : (iq + 1) * 32, v * 128 : (v + 1) * 128] = block.astype(BF16)
    gate_ref[...] = sigmoid(contract(normed_ref[...], og_ref[...], 1, 0))
    mix_half(0, left_ref, mine_ref, theirs_ref, spread_ref, sent_ref, slots_ref)


def far_kernel(left_ref, mine_ref, theirs_ref, spread_ref, half_ref, sent_ref, slots_ref):
    del half_ref
    mix_half(1, left_ref, mine_ref, theirs_ref, spread_ref, sent_ref, slots_ref)


def update_kernel(got_ref, gate_ref, columns_ref, weight_ref, out_ref, rows_ref, flat_ref):
    rows, cols, width = out_ref.shape
    gain = columns_ref[0][:, 0:1]
    bias = columns_ref[1][:, 0:1]
    for iq in range(3):
        rows_ref[iq] = got_ref[:, :, iq * 128 : (iq + 1) * 128].astype(F32).reshape(2 * width, 128)
        mixed = rows_ref[iq, pl.ds(0, width, stride=2), :] + rows_ref[iq, pl.ds(1, width, stride=2), :]
        mean = jnp.mean(mixed, axis=0, keepdims=True)
        centered = mixed - mean
        variance = jnp.mean(centered * centered, axis=0, keepdims=True)
        normed = (centered * lax.rsqrt(variance + EPS) * gain + bias).astype(BF16)
        output = contract(normed, weight_ref[...], 0, 0)
        for ii in range(4):
            at = (3 * ii + iq) * cols
            flat_ref[at : at + 12, :] = output[ii * WIDE : ii * WIDE + 12]
            flat_ref[at + 12 : at + 24, :] = output[ii * WIDE + 16 : ii * WIDE + 28]
    out_ref[...] = (gate_ref[...] * flat_ref[...]).astype(BF16).reshape(rows, cols, width)


def shards(
    pair,
    token_mask,
    norm_in_gain,
    norm_in_bias,
    left_gate,
    left_value,
    right_gate,
    right_value,
    output_gate,
    norm_out_gain,
    norm_out_bias,
    output_weight,
):
    rows, cols, width = pair.shape
    params = pltpu.CompilerParams(vmem_limit_bytes=32 * 1024 * 1024)
    struct = jax.ShapeDtypeStruct
    message = struct((width, 2, rows * WIDE), BF16)
    arrays = [pair.reshape(rows * cols, width), token_mask]
    arrays += [v.reshape(1, -1) for v in (norm_in_gain, norm_in_bias, norm_out_gain, norm_out_bias)]
    arrays += [left_gate, left_value, right_gate, right_value]
    fetched = [pltpu.VMEM(array.shape, array.dtype) for array in arrays]
    fetched[1] = pltpu.SMEM(token_mask.shape, token_mask.dtype)
    sent, normed, columns, spread = pl.pallas_call(
        edges_kernel,
        name="edges",
        out_shape=(
            message,
            struct((rows * cols, width), BF16),
            struct((2, width, width), F32),
            struct((192, 256), BF16),
        ),
        in_specs=[HBM] * 10,
        out_specs=(VMEM,) * 4,
        scratch_shapes=fetched + [pltpu.VMEM((3, 256, 128), F32), pltpu.SemaphoreType.DMA((10,))],
        compiler_params=params,
    )(*[pltpu.with_memory_space_constraint(array, pltpu.HBM) for array in arrays])
    got = lax.all_to_all(sent, BOTH, 0, 0, axis_index_groups=SHARING)
    scratch = [pltpu.VMEM((3, 256, 128), F32), pltpu.VMEM((384, 128), F32)]
    right = pl.pallas_call(
        right_kernel,
        name="right",
        out_shape=struct((96, 384), BF16),
        in_specs=[VMEM],
        out_specs=VMEM,
        scratch_shapes=scratch + [pltpu.VMEM((3, 96, 128), F32)],
        compiler_params=params,
    )(got)
    near = lax.ppermute(right, BOTH, CORE_FLIP)
    far = lax.ppermute(right, BOTH, HALF_FLIP)
    both = lax.ppermute(far, BOTH, CORE_FLIP)
    sent, gate, left = pl.pallas_call(
        near_kernel,
        name="near",
        out_shape=(message, struct((rows * cols, width), F32), struct((96, 384), BF16)),
        in_specs=[VMEM] * 6,
        out_specs=(VMEM,) * 3,
        scratch_shapes=[pltpu.VMEM((6, 64, 128), F32)] + scratch,
        compiler_params=params,
    )(got, right, near, spread, normed, output_gate)
    sent = pl.pallas_call(
        far_kernel,
        name="far",
        out_shape=message,
        in_specs=[VMEM] * 5,
        out_specs=VMEM,
        scratch_shapes=[pltpu.VMEM((6, 64, 128), F32)],
        input_output_aliases={4: 0},
        compiler_params=params,
    )(left, far, both, spread, sent)
    got = lax.all_to_all(sent, BOTH, 0, 0, axis_index_groups=SHARING)
    return pl.pallas_call(
        update_kernel,
        name="update",
        out_shape=struct((rows, cols, width), BF16),
        in_specs=[VMEM] * 4,
        out_specs=VMEM,
        scratch_shapes=[pltpu.VMEM((3, 256, 128), F32), pltpu.VMEM((rows * cols, 128), F32)],
        compiler_params=params,
    )(got, gate, columns, output_weight)


def solution(mesh):
    placed = (P("ia", "ja", None),) + (P(),) * 11
    return jax.shard_map(shards, mesh=mesh, in_specs=placed, out_specs=P("ia", "ja", None), check_vma=False)
```
